128 devices in a mesh: col: 16 (over x, y), row: 8 (over z, core).
Axes of the slice: x: 4, y: 4, z: 4, core: 2. Of those that a mesh axis runs over, the one named last changes fastest.
Arguments:
- raw_counts: bfloat16 [512, 4096, 256], P('row', 'col'), may hold values from -35 to 60
- gain_class: int32 [512, 4096], P('row', 'col'), may hold values from 0 to 15
- good_pixels: int32 [512, 4096], P('row', 'col'), may hold values 0 or 1
- class_gains: float32 [16, 256], replicated, may hold values from 0.6 to 1.6
Outputs:
- whitened: bfloat16 [512, 4096, 256], P('row', 'col')
- noise_field: bfloat16 [512, 4096, 256], P('row', 'col')
- factor: float32 [256, 256], replicated
The draws below stay inside these ranges and needn't reach their ends.
All inputs are finite; a program needn't handle non-finite values. No bound on the sum of `good_pixels` on one device may be relied on, other than what follows from the above.
Results may differ from the reference program's by a relative error of at most 0.002.
Values sent between devices are 32-bit elements; how exact they have to be, the bound alone decides.
No kernel may reach another device: no remote copies, remote signals or barrier semaphores. Data moves between devices by JAX's collectives and lax.ppermute only.
A program may use at most 256 MiB of HBM per device.

```python
import math
import jax
import jax.numpy as jnp
from jax import lax

BANDS = 256
GAINS = 16
NROW = 512
NCOL = 4096


def draw_raw_counts(key, part):
    keys = jax.random.split(key, 6)
    rows_pos = jnp.arange(NROW, dtype=jnp.float32)[:, None, None]
    cols_pos = jnp.arange(NCOL, dtype=jnp.float32)[None, :, None]
    illumination = 1.0 + 2.0 * cols_pos / NCOL
    offset = jax.random.uniform(keys[0], (BANDS,), jnp.float32, 1.0, 3.0)
    amplitudes = jax.random.uniform(keys[1], (4, BANDS), jnp.float32, -1.0, 1.0)
    freqs = jax.random.uniform(keys[2], (4, 2), jnp.float32, 0.01, 0.05)
    phases = jax.random.uniform(keys[3], (4,), jnp.float32, 0.0, 2.0 * math.pi)
    signal = jnp.zeros((NROW, NCOL, BANDS), jnp.float32)
    for term in range(4):
        wave = jnp.cos(freqs[term, 0] * rows_pos + freqs[term, 1] * cols_pos + phases[term])
        signal = signal + wave * amplitudes[term]
    sigma = jnp.exp(jax.random.uniform(keys[4], (BANDS,), jnp.float32, math.log(0.3), 0.0))
    base = jax.random.truncated_normal(keys[5], -5.0, 5.0, (NROW, NCOL, BANDS), jnp.float32)
    noise = sigma * (base + 0.5 * jnp.roll(base, 1, axis=2))
    values = illumination * (offset + signal + noise)
    return values.astype(jnp.bfloat16)


def place_ends(entries, rng, low, top_value):
    longest = entries.shape.index(max(entries.shape))
    spots = []
    for shift in (0, 1):
        where = [jax.random.randint(jax.random.fold_in(rng, axis), (), 0, length) for axis, length in enumerate(entries.shape)]
        where[longest] = (where[longest] + shift) % entries.shape[longest]
        spots.append(tuple(where))
    return entries.at[spots[0]].set(low).at[spots[1]].set(top_value)


def setup_inputs(seed: int = 0) -> dict:
    streams_of = jax.random.split(jax.random.key(seed), 5)
    raw_counts = draw_raw_counts(jax.random.fold_in(streams_of[4], 71), 0)
    gain_class = place_ends(jax.random.randint(streams_of[1], (NROW, NCOL), 0, GAINS), jax.random.fold_in(streams_of[1], 1), 0, GAINS - 1).astype(jnp.int32)
    good_pixels = place_ends((jax.random.randint(streams_of[2], (NROW, NCOL), 0, 16) < 15).astype(jnp.int32), jax.random.fold_in(streams_of[2], 1), 0, 1)
    class_gains = jnp.clip(jnp.exp(jax.random.uniform(streams_of[3], (GAINS, BANDS), jnp.float32, math.log(0.6), math.log(1.6))), 0.6, 1.6)
    return {"raw_counts": raw_counts, "gain_class": gain_class, "good_pixels": good_pixels, "class_gains": class_gains}


def reference(raw_counts, gain_class, good_pixels, class_gains):
    valid = good_pixels.astype(jnp.float32)
    calibrated = raw_counts.astype(jnp.float32) * class_gains[gain_class]
    zero_row = jnp.zeros((1, NCOL, BANDS), jnp.float32)
    zero_col = jnp.zeros((NROW, 1, BANDS), jnp.float32)
    down_w = jnp.concatenate([valid[1:] * valid[:-1], jnp.zeros((1, NCOL), jnp.float32)], 0)
    right_w = jnp.concatenate([valid[:, 1:] * valid[:, :-1], jnp.zeros((NROW, 1), jnp.float32)], 1)
    down_diff = jnp.concatenate([calibrated[1:] - calibrated[:-1], zero_row], 0) * down_w[..., None]
    right_diff = jnp.concatenate([calibrated[:, 1:] - calibrated[:, :-1], zero_col], 1) * right_w[..., None]
    flat_down = down_diff.reshape(-1, BANDS)
    flat_right = right_diff.reshape(-1, BANDS)
    noise_sum = jnp.dot(flat_down.T, flat_down, precision=lax.Precision.HIGHEST)
    noise_sum = noise_sum + jnp.dot(flat_right.T, flat_right, precision=lax.Precision.HIGHEST)
    pairs = jnp.sum(down_w) + jnp.sum(right_w)
    noise_cov = noise_sum / (2.0 * pairs)
    count = jnp.sum(valid)
    mean = jnp.sum((calibrated * valid[..., None]).reshape(-1, BANDS), axis=0) / count
    lower = jnp.linalg.cholesky(noise_cov)
    identity = jnp.eye(BANDS, dtype=lower.dtype)
    inverse = lax.linalg.triangular_solve(lower, identity, left_side=True, lower=True)
    centred = (calibrated - mean) * valid[..., None]
    whitened = jnp.dot(centred, inverse.T, precision=lax.Precision.HIGHEST).astype(jnp.bfloat16)
    noise_field = jnp.dot(down_diff + right_diff, inverse.T, precision=lax.Precision.HIGHEST).astype(jnp.bfloat16)
    flat_white = whitened.reshape(-1, BANDS)
    gram = jnp.dot(flat_white.T.astype(jnp.float32), flat_white.astype(jnp.float32), preferred_element_type=jnp.float32) / count
    factor = jnp.linalg.cholesky(gram).T
    return (whitened, noise_field, factor)
```

```python
import jax
import jax.numpy as jnp
from jax import lax
from jax.experimental import pallas as pl
from jax.experimental.pallas import tpu as pltpu
from jax.sharding import PartitionSpec as P

STEP_ROWS = 8
CHUNK = 32
HALF = 128
HIGHEST = lax.Precision.HIGHEST
F32 = jnp.float32
BF16 = jnp.bfloat16


def over_pixels(left, right):
    return lax.dot_general(left, right, (((0,), (0,)), ((), ())), preferred_element_type=F32)


def exact(left, right, left_dim=1, right_dim=0):
    return lax.dot_general(
        left,
        right,
        (((left_dim,), (right_dim,)), ((), ())),
        precision=HIGHEST,
        preferred_element_type=F32,
    )


def split(value):
    high = value.astype(BF16)
    return high, (value - high.astype(F32)).astype(BF16)


def stacked_gains(gains):
    high = gains.astype(BF16)
    rest = gains - high.astype(F32)
    middle = rest.astype(BF16)
    low = (rest - middle.astype(F32)).astype(BF16)
    return jnp.concatenate([high, middle, low], 0)


def row_gains(classes, valid, gains, count):
    which = lax.rem(lax.broadcasted_iota(jnp.int32, (3 * count, classes.shape[1]), 0), count)
    onehot = jnp.where((which == classes) & (valid > 0), 1.0, 0.0).astype(BF16)
    return over_pixels(onehot, gains)


def as_column(row):
    return jnp.transpose(jnp.broadcast_to(row, (8, row.shape[1])))[:, :1]


def edges_kernel(row_ref, col_ref, class_ref, valid_ref, gains_ref, row_out, col_out):
    count = gains_ref.shape[0]
    gains = stacked_gains(gains_ref[...])
    cols = row_ref.shape[1]
    rows = col_ref.shape[0]
    calibrated = row_ref[0].astype(F32) * row_gains(class_ref[0:1, :], valid_ref[0:1, :], gains, count)
    row_out[0:cols, :] = calibrated
    row_out[cols:, :] = jnp.broadcast_to(valid_ref[0:1, :].astype(F32), (8, cols))
    which = lax.rem(lax.broadcasted_iota(jnp.int32, (rows, 3 * count), 1), count)
    first_valid = valid_ref[:, 0:1]
    onehot = jnp.where((which == class_ref[:, 0:1]) & (first_valid > 0), 1.0, 0.0).astype(BF16)
    gain_col = jnp.dot(onehot, gains, preferred_element_type=F32)
    channels = gain_col.shape[1]
    raw_col = col_ref[...].astype(F32)[:, 0, :]
    col_out[:, :channels] = raw_col * gain_col
    col_out[:, channels:] = jnp.broadcast_to(first_valid.astype(F32), (rows, 128))


def edges(raw_counts, gain_class, good_pixels, class_gains):
    rows, cols, channels = raw_counts.shape
    whole = lambda shape: pl.BlockSpec(shape, lambda i: (0,) * len(shape))
    return pl.pallas_call(
        edges_kernel,
        grid=(1,),
        in_specs=[
            whole((1, cols, channels)),
            whole((rows, 16, channels)),
            whole((rows, cols)),
            whole((rows, cols)),
            whole(class_gains.shape),
        ],
        out_specs=[whole((cols + 8, channels)), whole((rows, channels + 128))],
        out_shape=[
            jax.ShapeDtypeStruct((cols + 8, channels), F32),
            jax.ShapeDtypeStruct((rows, channels + 128), F32),
        ],
        name="edges",
    )(raw_counts, raw_counts, gain_class, good_pixels, class_gains)


def moments_kernel(
    raw_ref, class_ref, valid_ref, gains_ref, high_ref, low_ref, products_ref, sums_ref, pivot_ref, plain, half_degree, terms, gains_bf
):
    step = pl.program_id(0)
    count = gains_ref.shape[0]
    rows, cols = valid_ref.shape
    channels = raw_ref.shape[2]

    @pl.when(step == 0)
    def _():
        valid = valid_ref[...].astype(F32)
        zero_row = jnp.zeros((1, cols), F32)
        zero_col = jnp.zeros((rows, 1), F32)
        degree = jnp.concatenate([valid[1:], zero_row], 0) + jnp.concatenate([zero_row, valid[:-1]], 0)
        degree = degree + jnp.concatenate([valid[:, 1:], zero_col], 1) + jnp.concatenate([zero_col, valid[:, :-1]], 1)
        half_degree[...] = 0.5 * degree
        plain[...] = jnp.zeros_like(plain)
        products_ref[...] = jnp.zeros_like(products_ref)
        sums_ref[...] = jnp.zeros_like(sums_ref)
        gains_bf[...] = stacked_gains(gains_ref[...])
        gain_map = row_gains(class_ref[0:1, :], valid_ref[0:1, :], gains_bf[...], count)
        number = jnp.maximum(jnp.sum(valid[0:1, :], keepdims=True), 1.0)
        pivot = jnp.sum(raw_ref[0].astype(F32) * gain_map, 0, keepdims=True) / number
        pivot_ref[...] = jnp.broadcast_to(pivot, pivot_ref.shape)

    start = pl.multiple_of(step * STEP_ROWS, STEP_ROWS)
    classes = class_ref[pl.ds(start, STEP_ROWS), :]
    valid = valid_ref[pl.ds(start, STEP_ROWS), :]
    degrees = jnp.transpose(half_degree[pl.ds(start, STEP_ROWS), :])
    valid_cols = jnp.transpose(valid.astype(F32))
    pivot = pivot_ref[0:1, :]
    gains = gains_bf[...]
    total = sums_ref[...]
    for row in range(STEP_ROWS):
        gain_map = row_gains(classes[row : row + 1], valid[row : row + 1], gains, count)
        for at in range(0, cols, CHUNK):
            calibrated = raw_ref[row, at : at + CHUNK, :].astype(F32) * gain_map[at : at + CHUNK]
            calibrated = calibrated - valid_cols[at : at + CHUNK, row : row + 1] * pivot
            high, low = split(calibrated)
            high_ref[row, at : at + CHUNK, :] = high
            low_ref[row, at : at + CHUNK, :] = low
            plain[row % 2, 8 + at : 8 + at + CHUNK, :] = calibrated
            left = plain[row % 2, 7 + at : 7 + at + CHUNK, :]
            above = plain[1 - row % 2, 8 + at : 8 + at + CHUNK, :]
            term = above + left - degrees[at : at + CHUNK, row : row + 1] * calibrated
            terms[row * cols + at : row * cols + at + CHUNK, :] = term.astype(BF16)
            total = total + jnp.sum(calibrated.reshape(CHUNK // 8, 8, channels), 0)
    sums_ref[...] = total
    pixels = STEP_ROWS * cols
    high = high_ref[...].reshape(pixels, channels)
    products_ref[...] += over_pixels(high, jnp.concatenate([terms[...], high], 1))


def moments(raw_counts, gain_class, good_pixels, class_gains):
    rows, cols, channels = raw_counts.shape
    whole = lambda shape: pl.BlockSpec(shape, lambda i: (0,) * len(shape))
    block = pl.BlockSpec((STEP_ROWS, cols, channels), lambda i: (i, 0, 0))
    pixels = rows * cols
    return pl.pallas_call(
        moments_kernel,
        grid=(rows // STEP_ROWS,),
        in_specs=[block, whole((rows, cols)), whole((rows, cols)), whole(class_gains.shape)],
        out_specs=[block, block, whole((channels, 2 * channels)), whole((8, channels)), whole((8, channels))],
        out_shape=[
            pltpu.HBM(raw_counts.shape, BF16),
            pltpu.HBM(raw_counts.shape, BF16),
            jax.ShapeDtypeStruct((channels, 2 * channels), F32),
            jax.ShapeDtypeStruct((8, channels), F32),
            jax.ShapeDtypeStruct((8, channels), F32),
        ],
        scratch_shapes=[
            pltpu.VMEM((2, 8 + cols, channels), F32),
            pltpu.VMEM((rows, cols), F32),
            pltpu.VMEM((STEP_ROWS * cols, channels), BF16),
            pltpu.VMEM((3 * class_gains.shape[0], channels), BF16),
        ],
        compiler_params=pltpu.CompilerParams(vmem_limit_bytes=32 * 1024 * 1024),
        cost_estimate=pl.CostEstimate(
            flops=10 * pixels * channels * channels, bytes_accessed=6 * pixels * channels, transcendentals=0
        ),
        name="moments",
    )(raw_counts, gain_class, good_pixels, class_gains)


def pack_kernel(
    products_ref, sums_ref, pivot_ref, below_ref, right_ref, high_row, low_row, high_col, low_col, valid_ref, packed_ref
):
    rows, cols = valid_ref.shape
    channels = sums_ref.shape[1]
    valid = valid_ref[...].astype(F32)
    last_valid = as_column(valid[rows - 1 : rows, :])
    below_row = below_ref[cols : cols + 1, :]
    below_valid = as_column(below_row)
    mine = high_row[0].astype(F32) + low_row[0].astype(F32)
    pivot = pivot_ref[0:1, :]
    down = last_valid * (below_ref[0:cols, :] - below_valid * pivot) - below_valid * mine
    right_valid = right_ref[:, channels : channels + 1]
    mine = (high_col[...].astype(F32) + low_col[...].astype(F32))[:, 15, :]
    last_col = valid[:, cols - 1 : cols]
    right = last_col * (right_ref[:, :channels] - right_valid * pivot) - right_valid * mine
    edge = jnp.concatenate([down, right], 0).astype(BF16)
    cross = products_ref[:, :channels]
    noise = over_pixels(edge, edge) - (cross + jnp.transpose(cross))
    number = jnp.sum(valid, keepdims=True)
    total = jnp.sum(sums_ref[...], 0, keepdims=True)
    shift = total + number * pivot
    second = products_ref[:, channels:] + (as_column(pivot) * shift + as_column(total) * pivot)
    total = shift
    at = 0
    for matrix in (noise, second):
        for part in (matrix[:HALF, :HALF], matrix[:HALF, HALF:], matrix[HALF:, HALF:]):
            packed_ref[at : at + HALF, :] = part
            at += HALF
    pairs = jnp.sum(valid[1:] * valid[:-1], keepdims=True) + jnp.sum(valid[:, 1:] * valid[:, :-1], keepdims=True)
    pairs = pairs + jnp.sum(valid[rows - 1 :] * below_row, keepdims=True)
    pairs = pairs + jnp.sum(last_col * right_valid, keepdims=True)
    line = lax.broadcasted_iota(jnp.int32, (8, HALF), 0)
    packed_ref[at : at + 8, :] = jnp.where(
        line == 0,
        total[:, :HALF],
        jnp.where(line == 1, total[:, HALF:], jnp.where(line == 2, number, jnp.where(line == 3, pairs, 0.0))),
    )
    packed_ref[at + 8 :, :] = jnp.zeros((packed_ref.shape[0] - at - 8, HALF), F32)


def pack(products, sums, pivot, below, right, high, low, good_pixels, length):
    rows, cols, channels = high.shape
    whole = lambda shape: pl.BlockSpec(shape, lambda i: (0,) * len(shape))
    last_row = pl.BlockSpec((1, cols, channels), lambda i: (rows - 1, 0, 0))
    last_col = pl.BlockSpec((rows, 16, channels), lambda i: (0, cols // 16 - 1, 0))
    return pl.pallas_call(
        pack_kernel,
        grid=(1,),
        in_specs=[
            whole(products.shape),
            whole(sums.shape),
            whole(pivot.shape),
            whole(below.shape),
            whole(right.shape),
            last_row,
            last_row,
            last_col,
            last_col,
            whole((rows, cols)),
        ],
        out_specs=whole((length, HALF)),
        out_shape=jax.ShapeDtypeStruct((length, HALF), F32),
        compiler_params=pltpu.CompilerParams(vmem_limit_bytes=32 * 1024 * 1024),
        name="pack",
    )(products, sums, pivot, below, right, high, low, high, low, good_pixels)


def inverse_of_pair(a, b, c):
    scale = 1.0 / (a * c - b * b)
    return c * scale, -(b * scale), a * scale


def eliminate(jobs):
    lane = lax.broadcasted_iota(jnp.int32, (8, HALF), 1)
    line = lax.broadcasted_iota(jnp.int32, (8, HALF), 0)
    spread = lambda value: jnp.broadcast_to(value, (8, HALF))
    pick = lambda value, place: jnp.take_along_axis(
        value, jnp.full((8, HALF), place, jnp.int32), axis=1, mode="promise_in_bounds"
    )
    tiles = HALF // 8
    done = [([None] * tiles, [None] * tiles) for _ in jobs]
    for turn in range(HALF // 4):
        tile, first, at = turn // 2, 4 * (turn % 2), 4 * turn
        for job, (done_main, done_extra) in zip(jobs, done):
            main, extra = job["main"], job["extra"]
            lead = main[tile]
            rows = [spread(lead[first + i : first + i + 1, :]) for i in range(4)]
            p = {(i, j): pick(rows[i], at + j) for i in range(4) for j in range(i, 4)}
            if job["inverse"]:
                inside = (lane >= at) & (lane < at + 4)
                rows = [jnp.where(inside, jnp.where(lane == at + i, 1.0, 0.0), row) for i, row in enumerate(rows)]
            more = [spread(extra[tile][first + i : first + i + 1, :]) for i in range(4)] if extra else None
            e00, e01, e11 = inverse_of_pair(p[0, 0], p[0, 1], p[1, 1])
            f00 = e00 * p[0, 2] + e01 * p[1, 2]
            f10 = e01 * p[0, 2] + e11 * p[1, 2]
            f01 = e00 * p[0, 3] + e01 * p[1, 3]
            f11 = e01 * p[0, 3] + e11 * p[1, 3]
            g00, g01, g11 = inverse_of_pair(
                p[2, 2] - (p[0, 2] * f00 + p[1, 2] * f10),
                p[2, 3] - (p[0, 2] * f01 + p[1, 2] * f11),
                p[3, 3] - (p[0, 3] * f01 + p[1, 3] * f11),
            )
            i0 = lax.rsqrt(p[0, 0])
            l10, l20, l30 = p[0, 1] * i0, p[0, 2] * i0, p[0, 3] * i0
            i1 = lax.rsqrt(p[1, 1] - l10 * l10)
            l21, l31 = (p[1, 2] - l20 * l10) * i1, (p[1, 3] - l30 * l10) * i1
            i2 = lax.rsqrt(p[2, 2] - (l20 * l20 + l21 * l21))
            l32 = (p[2, 3] - (l30 * l20 + l31 * l21)) * i2
            i3 = lax.rsqrt(p[3, 3] - (l30 * l30 + l31 * l31 + l32 * l32))
            solved = []
            for group, target in ((rows, done_main), (more, done_extra)):
                if group is None:
                    solved.append(None)
                    continue
                u2 = group[2] - (f00 * group[0] + f10 * group[1])
                u3 = group[3] - (f01 * group[0] + f11 * group[1])
                z2 = g00 * u2 + g01 * u3
                z3 = g01 * u2 + g11 * u3
                z0 = (e00 * group[0] + e01 * group[1]) - (f00 * z2 + f01 * z3)
                z1 = (e01 * group[0] + e11 * group[1]) - (f10 * z2 + f11 * z3)
                solved.append((z0, z1, z2, z3))
                r0 = group[0] * i0
                r1 = (group[1] - l10 * r0) * i1
                r2 = (group[2] - (l20 * r0 + l21 * r1)) * i2
                r3 = (group[3] - (l30 * r0 + l31 * r1 + l32 * r2)) * i3
                quad = jnp.where(
                    line == first,
                    r0,
                    jnp.where(line == first + 1, r1, jnp.where(line == first + 2, r2, r3)),
                )
                target[tile] = quad if first == 0 else jnp.where(line < 4, target[tile], quad)
            for j in range(tile if first == 0 else tile + 1, tiles):
                weights = [spread(main[j][:, at + i : at + i + 1]) for i in range(4)]
                if j == tile:
                    weights = [jnp.where(line >= 4, weight, 0.0) for weight in weights]
                base = jnp.where(inside, 0.0, main[j]) if job["inverse"] else main[j]
                z = solved[0]
                main[j] = base - (
                    (weights[0] * z[0] + weights[1] * z[1]) + (weights[2] * z[2] + weights[3] * z[3])
                )
                if extra:
                    z = solved[1]
                    extra[j] = extra[j] - (
                        (weights[0] * z[0] + weights[1] * z[1]) + (weights[2] * z[2] + weights[3] * z[3])
                    )
    row = lax.broadcasted_iota(jnp.int32, (HALF, HALF), 0)
    col = lax.broadcasted_iota(jnp.int32, (HALF, HALF), 1)
    results = []
    for job, (done_main, done_extra) in zip(jobs, done):
        main = jnp.concatenate(done_main, 0)
        keep = (col <= row) if job["inverse"] else (col >= row)
        main = jnp.where(keep, main, 0.0)
        results.append((main, jnp.concatenate(done_extra, 0) if job["extra"] else None))
    return results


def tiles_of(matrix):
    return [matrix[8 * i : 8 * i + 8, :] for i in range(HALF // 8)]


def factors(packed_ref, pivot_ref, weights_ref, offset_ref, factor_ref):
    channels = 2 * HALF
    base = 6 * HALF
    line0 = packed_ref[base : base + 8, :]
    number = jnp.broadcast_to(line0[2:3, 0:1], (1, HALF))
    pairs = jnp.broadcast_to(line0[3:4, 0:1], (1, HALF))
    noise_scale = 1.0 / (2.0 * pairs)
    scale = 1.0 / number
    mean0, mean1 = line0[0:1] * scale, line0[1:2] * scale
    column0 = as_column(mean0)
    column1 = as_column(mean1)
    part = lambda i: packed_ref[HALF * i : HALF * (i + 1), :]
    n00, n01, n11 = part(0) * noise_scale, part(1) * noise_scale, part(2) * noise_scale
    s00 = part(3) * scale - column0 * mean0
    s01 = part(4) * scale - column0 * mean1
    s11 = part(5) * scale - column1 * mean1
    (w00, y), (k00, k01) = eliminate(
        [
            dict(main=tiles_of(n00), extra=tiles_of(n01), inverse=True),
            dict(main=tiles_of(s00), extra=tiles_of(s01), inverse=False),
        ]
    )
    n11 = n11 - exact(y, y, 0, 0)
    s11 = s11 - exact(k01, k01, 0, 0)
    (w11, _), (k11, _) = eliminate(
        [
            dict(main=tiles_of(n11), extra=None, inverse=True),
            dict(main=tiles_of(s11), extra=None, inverse=False),
        ]
    )
    w10 = -exact(w11, exact(y, w00, 0, 0))
    factor_ref[:HALF, :HALF] = exact(k00, w00, 1, 1)
    factor_ref[:HALF, HALF:] = exact(k00, w10, 1, 1) + exact(k01, w11, 1, 1)
    factor_ref[HALF:, :HALF] = jnp.zeros((HALF, HALF), F32)
    factor_ref[HALF:, HALF:] = exact(k11, w11, 1, 1)
    mean0 = jnp.broadcast_to(mean0, (8, HALF)) - pivot_ref[:, :HALF]
    mean1 = jnp.broadcast_to(mean1, (8, HALF)) - pivot_ref[:, HALF:]
    offset_ref[:, :HALF] = exact(mean0, w00, 1, 1)
    offset_ref[:, HALF:] = exact(mean0, w10, 1, 1) + exact(mean1, w11, 1, 1)
    left = jnp.concatenate([jnp.transpose(w00), jnp.zeros((HALF, HALF), F32)], 0)
    right = jnp.concatenate([jnp.transpose(w10), jnp.transpose(w11)], 0)
    high, low = split(jnp.concatenate([left, right], 1))
    weights_ref[0:channels, :] = high
    weights_ref[channels : 2 * channels, :] = low
    weights_ref[2 * channels :, :] = high


def whiten_rows(high, low, weights):
    return jnp.dot(jnp.concatenate([high, high, low], 1), weights, preferred_element_type=F32)


def whiten_kernel(
    packed_ref,
    pivot_ref,
    high_from,
    low_from,
    valid_ref,
    below_ref,
    right_ref,
    white_ref,
    noise_ref,
    factor_ref,
    high_ref,
    low_ref,
    weights_ref,
    offset_ref,
    plain,
    right_edge,
    neighbours,
    arrived,
):
    step = pl.program_id(0)
    steps = pl.num_programs(0)
    rows, cols = valid_ref.shape
    channels = high_ref.shape[2]

    @pl.when(step == 0)
    def _():
        valid = valid_ref[...].astype(F32)
        down = jnp.concatenate([valid[1:], below_ref[cols : cols + 1, :]], 0)
        right = jnp.concatenate([valid[:, 1:], right_ref[:, channels : channels + 1]], 1)
        neighbours[...] = down + right
        copies = [
            pltpu.make_async_copy(high_from, high_ref, arrived.at[0]),
            pltpu.make_async_copy(low_from, low_ref, arrived.at[1]),
        ]
        for copy in copies:
            copy.start()
        factors(packed_ref, pivot_ref, weights_ref, offset_ref, factor_ref)
        pivot = pivot_ref[0:1, :]
        below = below_ref[0:cols, :] - as_column(below_ref[cols : cols + 1, :]) * pivot
        plain[STEP_ROWS * (cols + 8) :, :] = whiten_rows(*split(below), weights_ref[...])
        right = right_ref[:, :channels] - right_ref[:, channels : channels + 1] * pivot
        right_edge[...] = whiten_rows(*split(right), weights_ref[...])
        for copy in copies:
            copy.wait()

    start = pl.multiple_of((steps - 1 - step) * STEP_ROWS, STEP_ROWS)
    valid = jnp.transpose(valid_ref[pl.ds(start, STEP_ROWS), :].astype(F32))
    number = jnp.transpose(neighbours[pl.ds(start, STEP_ROWS), :])
    edge = right_edge[pl.ds(start, STEP_ROWS), :]
    offset = offset_ref[0:1, :]
    weights = weights_ref[...]
    for row in reversed(range(STEP_ROWS)):
        base = row * (cols + 8)
        plain[base : base + cols, :] = whiten_rows(high_ref[start + row], low_ref[start + row], weights)
        plain[base + cols : base + cols + 1, :] = edge[row : row + 1]
        for at in range(0, cols, CHUNK):
            here = plain[base + at : base + at + CHUNK, :]
            right = plain[base + at + 1 : base + at + 1 + CHUNK, :]
            below = plain[base + cols + 8 + at : base + cols + 8 + at + CHUNK, :]
            ok = valid[at : at + CHUNK, row : row + 1]
            white_ref[row, at : at + CHUNK, :] = (here - ok * offset).astype(BF16)
            around = number[at : at + CHUNK, row : row + 1]
            noise_ref[row, at : at + CHUNK, :] = (ok * (below + right) - around * here).astype(BF16)
    plain[STEP_ROWS * (cols + 8) :, :] = plain[0 : cols, :]


def whiten(packed, pivot, high, low, good_pixels, below, right):
    rows, cols, channels = high.shape
    steps = rows // STEP_ROWS
    pixels = rows * cols
    whole = lambda shape: pl.BlockSpec(shape, lambda i: (0,) * len(shape))
    block = pl.BlockSpec((STEP_ROWS, cols, channels), lambda i: (steps - 1 - i, 0, 0))
    return pl.pallas_call(
        whiten_kernel,
        grid=(steps,),
        in_specs=[
            whole(packed.shape),
            whole(pivot.shape),
            pl.BlockSpec(memory_space=pl.ANY),
            pl.BlockSpec(memory_space=pl.ANY),
            whole((rows, cols)),
            whole(below.shape),
            whole(right.shape),
        ],
        out_specs=[block, block, whole((channels, channels))],
        out_shape=[jax.ShapeDtypeStruct(high.shape, BF16)] * 2 + [jax.ShapeDtypeStruct((channels, channels), F32)],
        scratch_shapes=[
            pltpu.VMEM(high.shape, BF16),
            pltpu.VMEM(low.shape, BF16),
            pltpu.VMEM((3 * channels, channels), BF16),
            pltpu.VMEM((8, channels), F32),
            pltpu.VMEM((STEP_ROWS * (cols + 8) + cols, channels), F32),
            pltpu.VMEM((rows, channels), F32),
            pltpu.VMEM((rows, cols), F32),
            pltpu.SemaphoreType.DMA((2,)),
        ],
        compiler_params=pltpu.CompilerParams(vmem_limit_bytes=48 * 1024 * 1024),
        cost_estimate=pl.CostEstimate(
            flops=6 * pixels * channels * channels, bytes_accessed=8 * pixels * channels, transcendentals=0
        ),
        name="whiten",
    )(packed, pivot, high, low, good_pixels, below, right)


def from_next(value, axis):
    count = lax.axis_size(axis)
    return lax.ppermute(value, axis, [(source, source - 1) for source in range(1, count)])


def summed(packed, axes):
    devices = lax.axis_size(axes)
    share = packed.reshape(devices, packed.shape[0] // devices, HALF)
    mine = jnp.sum(lax.all_to_all(share, axes, 0, 0), 0)
    every = lax.all_to_all(jnp.broadcast_to(mine[None], share.shape), axes, 0, 0)
    return every.reshape(packed.shape)


def on_device(raw_counts, gain_class, good_pixels, class_gains):
    axes = ("col", "row")
    raw_counts = pltpu.with_memory_space_constraint(raw_counts, pltpu.HBM)
    first_row, first_col = edges(raw_counts, gain_class, good_pixels, class_gains)
    below = from_next(first_row, "row")
    right = from_next(first_col, "col")
    high, low, products, sums, pivot = moments(raw_counts, gain_class, good_pixels, class_gains)
    high, low = (pltpu.with_memory_space_constraint(part, pltpu.HBM) for part in (high, low))
    devices = lax.axis_size(axes)
    length = -(-(6 * HALF + 8) // (8 * devices)) * 8 * devices
    packed = pack(products, sums, pivot, below, right, high, low, good_pixels, length)
    return whiten(summed(packed, axes), pivot, high, low, good_pixels, below, right)


def solution(mesh):
    return jax.shard_map(
        on_device,
        mesh=mesh,
        in_specs=(P("row", "col", None), P("row", "col"), P("row", "col"), P()),
        out_specs=(P("row", "col", None), P("row", "col", None), P()),
        check_vma=False,
    )
```

```python
import jax
import jax.numpy as jnp
from jax import lax
from jax.experimental import pallas as pl
from jax.experimental.pallas import tpu as pltpu
from jax.sharding import PartitionSpec as P

STEP_ROWS = 16
CHUNK = 32
HALF = 128
HIGHEST = lax.Precision.HIGHEST
F32 = jnp.float32
BF16 = jnp.bfloat16


def over_pixels(left, right):
    return lax.dot_general(left, right, (((0,), (0,)), ((), ())), preferred_element_type=F32)


def exact(left, right, left_dim=1, right_dim=0):
    return lax.dot_general(
        left,
        right,
        (((left_dim,), (right_dim,)), ((), ())),
        precision=HIGHEST,
        preferred_element_type=F32,
    )


def split(value):
    high = value.astype(BF16)
    return high, (value - high.astype(F32)).astype(BF16)


def stacked_gains(gains):
    high = gains.astype(BF16)
    rest = gains - high.astype(F32)
    middle = rest.astype(BF16)
    low = (rest - middle.astype(F32)).astype(BF16)
    return jnp.concatenate([high, middle, low], 0)


def row_gains(classes, valid, gains, count):
    which = lax.rem(lax.broadcasted_iota(jnp.int32, (3 * count, classes.shape[1]), 0), count)
    onehot = jnp.where((which == classes) & (valid > 0), 1.0, 0.0).astype(BF16)
    return over_pixels(onehot, gains)


def as_column(row):
    return jnp.transpose(jnp.broadcast_to(row, (8, row.shape[1])))[:, :1]


def edges_kernel(row_ref, col_ref, class_ref, valid_ref, gains_ref, row_out, col_out):
    count = gains_ref.shape[0]
    gains = stacked_gains(gains_ref[...])
    cols = row_ref.shape[1]
    rows = col_ref.shape[0]
    calibrated = row_ref[0].astype(F32) * row_gains(class_ref[0:1, :], valid_ref[0:1, :], gains, count)
    row_out[0:cols, :] = calibrated
    row_out[cols:, :] = jnp.broadcast_to(valid_ref[0:1, :].astype(F32), (8, cols))
    which = lax.rem(lax.broadcasted_iota(jnp.int32, (rows, 3 * count), 1), count)
    first_valid = valid_ref[:, 0:1]
    onehot = jnp.where((which == class_ref[:, 0:1]) & (first_valid > 0), 1.0, 0.0).astype(BF16)
    gain_col = jnp.dot(onehot, gains, preferred_element_type=F32)
    channels = gain_col.shape[1]
    raw_col = col_ref[...].astype(F32)[:, 0, :]
    col_out[:, :channels] = raw_col * gain_col
    col_out[:, channels:] = jnp.broadcast_to(first_valid.astype(F32), (rows, 128))


def edges(raw_counts, gain_class, good_pixels, class_gains):
    rows, cols, channels = raw_counts.shape
    whole = lambda shape: pl.BlockSpec(shape, lambda i: (0,) * len(shape))
    return pl.pallas_call(
        edges_kernel,
        grid=(1,),
        in_specs=[
            whole((1, cols, channels)),
            whole((rows, 16, channels)),
            whole((rows, cols)),
            whole((rows, cols)),
            whole(class_gains.shape),
        ],
        out_specs=[whole((cols + 8, channels)), whole((rows, channels + 128))],
        out_shape=[
            jax.ShapeDtypeStruct((cols + 8, channels), F32),
            jax.ShapeDtypeStruct((rows, channels + 128), F32),
        ],
        name="edges",
    )(raw_counts, raw_counts, gain_class, good_pixels, class_gains)


def moments_kernel(
    raw_ref, class_ref, valid_ref, gains_ref, high_ref, low_ref, products_ref, sums_ref, pivot_ref, plain, half_degree, terms, gains_bf
):
    step = pl.program_id(0)
    count = gains_ref.shape[0]
    rows, cols = valid_ref.shape
    channels = raw_ref.shape[2]

    @pl.when(step == 0)
    def _():
        valid = valid_ref[...].astype(F32)
        zero_row = jnp.zeros((1, cols), F32)
        zero_col = jnp.zeros((rows, 1), F32)
        degree = jnp.concatenate([valid[1:], zero_row], 0) + jnp.concatenate([zero_row, valid[:-1]], 0)
        degree = degree + jnp.concatenate([valid[:, 1:], zero_col], 1) + jnp.concatenate([zero_col, valid[:, :-1]], 1)
        half_degree[...] = 0.5 * degree
        plain[...] = jnp.zeros_like(plain)
        products_ref[...] = jnp.zeros_like(products_ref)
        sums_ref[...] = jnp.zeros_like(sums_ref)
        gains_bf[...] = stacked_gains(gains_ref[...])
        gain_map = row_gains(class_ref[0:1, :], valid_ref[0:1, :], gains_bf[...], count)
        number = jnp.maximum(jnp.sum(valid[0:1, :], keepdims=True), 1.0)
        pivot = jnp.sum(raw_ref[0].astype(F32) * gain_map, 0, keepdims=True) / number
        pivot_ref[...] = jnp.broadcast_to(pivot, pivot_ref.shape)

    start = pl.multiple_of(step * STEP_ROWS, STEP_ROWS)
    classes = class_ref[pl.ds(start, STEP_ROWS), :]
    valid = valid_ref[pl.ds(start, STEP_ROWS), :]
    degrees = jnp.transpose(half_degree[pl.ds(start, STEP_ROWS), :])
    valid_cols = jnp.transpose(valid.astype(F32))
    pivot = pivot_ref[0:1, :]
    gains = gains_bf[...]
    total = sums_ref[...]
    for row in range(STEP_ROWS):
        gain_map = row_gains(classes[row : row + 1], valid[row : row + 1], gains, count)
        for at in range(0, cols, CHUNK):
            calibrated = raw_ref[row, at : at + CHUNK, :].astype(F32) * gain_map[at : at + CHUNK]
            calibrated = calibrated - valid_cols[at : at + CHUNK, row : row + 1] * pivot
            high, low = split(calibrated)
            high_ref[row, at : at + CHUNK, :] = high
            low_ref[row, at : at + CHUNK, :] = low
            plain[row % 2, 8 + at : 8 + at + CHUNK, :] = calibrated
            left = plain[row % 2, 7 + at : 7 + at + CHUNK, :]
            above = plain[1 - row % 2, 8 + at : 8 + at + CHUNK, :]
            term = above + left - degrees[at : at + CHUNK, row : row + 1] * calibrated
            terms[row * cols + at : row * cols + at + CHUNK, :] = term.astype(BF16)
            total = total + jnp.sum(calibrated.reshape(CHUNK // 8, 8, channels), 0)
    sums_ref[...] = total
    pixels = STEP_ROWS * cols
    high = high_ref[...].reshape(pixels, channels)
    products_ref[...] += over_pixels(high, jnp.concatenate([terms[...], high], 1))


def moments(raw_counts, gain_class, good_pixels, class_gains):
    rows, cols, channels = raw_counts.shape
    whole = lambda shape: pl.BlockSpec(shape, lambda i: (0,) * len(shape))
    block = pl.BlockSpec((STEP_ROWS, cols, channels), lambda i: (i, 0, 0))
    pixels = rows * cols
    return pl.pallas_call(
        moments_kernel,
        grid=(rows // STEP_ROWS,),
        in_specs=[block, whole((rows, cols)), whole((rows, cols)), whole(class_gains.shape)],
        out_specs=[block, block, whole((channels, 2 * channels)), whole((8, channels)), whole((8, channels))],
        out_shape=[
            pltpu.HBM(raw_counts.shape, BF16),
            pltpu.HBM(raw_counts.shape, BF16),
            jax.ShapeDtypeStruct((channels, 2 * channels), F32),
            jax.ShapeDtypeStruct((8, channels), F32),
            jax.ShapeDtypeStruct((8, channels), F32),
        ],
        scratch_shapes=[
            pltpu.VMEM((2, 8 + cols, channels), F32),
            pltpu.VMEM((rows, cols), F32),
            pltpu.VMEM((STEP_ROWS * cols, channels), BF16),
            pltpu.VMEM((3 * class_gains.shape[0], channels), BF16),
        ],
        compiler_params=pltpu.CompilerParams(vmem_limit_bytes=32 * 1024 * 1024),
        cost_estimate=pl.CostEstimate(
            flops=10 * pixels * channels * channels, bytes_accessed=6 * pixels * channels, transcendentals=0
        ),
        name="moments",
    )(raw_counts, gain_class, good_pixels, class_gains)


def pack_kernel(
    products_ref, sums_ref, pivot_ref, below_ref, right_ref, high_row, low_row, high_col, low_col, valid_ref, packed_ref
):
    rows, cols = valid_ref.shape
    channels = sums_ref.shape[1]
    valid = valid_ref[...].astype(F32)
    last_valid = as_column(valid[rows - 1 : rows, :])
    below_row = below_ref[cols : cols + 1, :]
    below_valid = as_column(below_row)
    mine = high_row[0].astype(F32) + low_row[0].astype(F32)
    pivot = pivot_ref[0:1, :]
    down = last_valid * (below_ref[0:cols, :] - below_valid * pivot) - below_valid * mine
    right_valid = right_ref[:, channels : channels + 1]
    mine = (high_col[...].astype(F32) + low_col[...].astype(F32))[:, 15, :]
    last_col = valid[:, cols - 1 : cols]
    right = last_col * (right_ref[:, :channels] - right_valid * pivot) - right_valid * mine
    edge = jnp.concatenate([down, right], 0).astype(BF16)
    cross = products_ref[:, :channels]
    noise = over_pixels(edge, edge) - (cross + jnp.transpose(cross))
    number = jnp.sum(valid, keepdims=True)
    total = jnp.sum(sums_ref[...], 0, keepdims=True)
    shift = total + number * pivot
    second = products_ref[:, channels:] + (as_column(pivot) * shift + as_column(total) * pivot)
    total = shift
    row = lax.broadcasted_iota(jnp.int32, (HALF, HALF), 0)
    col = lax.broadcasted_iota(jnp.int32, (HALF, HALF), 1)
    at = 0
    diagonals = []
    for matrix in (noise, second):
        packed_ref[at : at + HALF, :] = jnp.where(col <= row, matrix[:HALF, :HALF], matrix[HALF:, HALF:])
        packed_ref[at + HALF : at + 2 * HALF, :] = matrix[:HALF, HALF:]
        diagonals.append(jnp.sum(jnp.where(row == col, matrix[HALF:, HALF:], 0.0), 0, keepdims=True))
        at += 2 * HALF
    pairs = jnp.sum(valid[1:] * valid[:-1], keepdims=True) + jnp.sum(valid[:, 1:] * valid[:, :-1], keepdims=True)
    pairs = pairs + jnp.sum(valid[rows - 1 :] * below_row, keepdims=True)
    pairs = pairs + jnp.sum(last_col * right_valid, keepdims=True)
    line = lax.broadcasted_iota(jnp.int32, (8, HALF), 0)
    packed_ref[at : at + 8, :] = jnp.where(
        line == 0,
        total[:, :HALF],
        jnp.where(
            line == 1,
            total[:, HALF:],
            jnp.where(
                line == 2,
                number,
                jnp.where(
                    line == 3, pairs, jnp.where(line == 4, diagonals[0], jnp.where(line == 5, diagonals[1], 0.0))
                ),
            ),
        ),
    )
    if packed_ref.shape[0] > at + 8:
        packed_ref[at + 8 :, :] = jnp.zeros((packed_ref.shape[0] - at - 8, HALF), F32)


def pack(products, sums, pivot, below, right, high, low, good_pixels, length):
    rows, cols, channels = high.shape
    whole = lambda shape: pl.BlockSpec(shape, lambda i: (0,) * len(shape))
    last_row = pl.BlockSpec((1, cols, channels), lambda i: (rows - 1, 0, 0))
    last_col = pl.BlockSpec((rows, 16, channels), lambda i: (0, cols // 16 - 1, 0))
    return pl.pallas_call(
        pack_kernel,
        grid=(1,),
        in_specs=[
            whole(products.shape),
            whole(sums.shape),
            whole(pivot.shape),
            whole(below.shape),
            whole(right.shape),
            last_row,
            last_row,
            last_col,
            last_col,
            whole((rows, cols)),
        ],
        out_specs=whole((length, HALF)),
        out_shape=jax.ShapeDtypeStruct((length, HALF), F32),
        compiler_params=pltpu.CompilerParams(vmem_limit_bytes=32 * 1024 * 1024),
        name="pack",
    )(products, sums, pivot, below, right, high, low, high, low, good_pixels)


def inverse_of_pair(a, b, c):
    scale = 1.0 / (a * c - b * b)
    return c * scale, -(b * scale), a * scale


def eliminate(jobs):
    lane = lax.broadcasted_iota(jnp.int32, (8, HALF), 1)
    line = lax.broadcasted_iota(jnp.int32, (8, HALF), 0)
    spread = lambda value: jnp.broadcast_to(value, (8, HALF))
    pick = lambda value, place: jnp.take_along_axis(
        value, jnp.full((8, HALF), place, jnp.int32), axis=1, mode="promise_in_bounds"
    )
    tiles = HALF // 8
    done = [([None] * tiles, [None] * tiles) for _ in jobs]
    for turn in range(HALF // 4):
        tile, first, at = turn // 2, 4 * (turn % 2), 4 * turn
        for job, (done_main, done_extra) in zip(jobs, done):
            main, extra = job["main"], job["extra"]
            lead = main[tile]
            rows = [spread(lead[first + i : first + i + 1, :]) for i in range(4)]
            p = {(i, j): pick(rows[i], at + j) for i in range(4) for j in range(i, 4)}
            if job["inverse"]:
                inside = (lane >= at) & (lane < at + 4)
                rows = [jnp.where(inside, jnp.where(lane == at + i, 1.0, 0.0), row) for i, row in enumerate(rows)]
            more = [spread(extra[tile][first + i : first + i + 1, :]) for i in range(4)] if extra else None
            e00, e01, e11 = inverse_of_pair(p[0, 0], p[0, 1], p[1, 1])
            f00 = e00 * p[0, 2] + e01 * p[1, 2]
            f10 = e01 * p[0, 2] + e11 * p[1, 2]
            f01 = e00 * p[0, 3] + e01 * p[1, 3]
            f11 = e01 * p[0, 3] + e11 * p[1, 3]
            g00, g01, g11 = inverse_of_pair(
                p[2, 2] - (p[0, 2] * f00 + p[1, 2] * f10),
                p[2, 3] - (p[0, 2] * f01 + p[1, 2] * f11),
                p[3, 3] - (p[0, 3] * f01 + p[1, 3] * f11),
            )
            i0 = lax.rsqrt(p[0, 0])
            l10, l20, l30 = p[0, 1] * i0, p[0, 2] * i0, p[0, 3] * i0
            i1 = lax.rsqrt(p[1, 1] - l10 * l10)
            l21, l31 = (p[1, 2] - l20 * l10) * i1, (p[1, 3] - l30 * l10) * i1
            i2 = lax.rsqrt(p[2, 2] - (l20 * l20 + l21 * l21))
            l32 = (p[2, 3] - (l30 * l20 + l31 * l21)) * i2
            i3 = lax.rsqrt(p[3, 3] - (l30 * l30 + l31 * l31 + l32 * l32))
            solved = []
            for group, target in ((rows, done_main), (more, done_extra)):
                if group is None:
                    solved.append(None)
                    continue
                u2 = group[2] - (f00 * group[0] + f10 * group[1])
                u3 = group[3] - (f01 * group[0] + f11 * group[1])
                z2 = g00 * u2 + g01 * u3
                z3 = g01 * u2 + g11 * u3
                z0 = (e00 * group[0] + e01 * group[1]) - (f00 * z2 + f01 * z3)
                z1 = (e01 * group[0] + e11 * group[1]) - (f10 * z2 + f11 * z3)
                solved.append((z0, z1, z2, z3))
                r0 = group[0] * i0
                r1 = (group[1] - l10 * r0) * i1
                r2 = (group[2] - (l20 * r0 + l21 * r1)) * i2
                r3 = (group[3] - (l30 * r0 + l31 * r1 + l32 * r2)) * i3
                quad = jnp.where(
                    line == first,
                    r0,
                    jnp.where(line == first + 1, r1, jnp.where(line == first + 2, r2, r3)),
                )
                target[tile] = quad if first == 0 else jnp.where(line < 4, target[tile], quad)
            for j in range(tile if first == 0 else tile + 1, tiles):
                weights = [spread(main[j][:, at + i : at + i + 1]) for i in range(4)]
                if j == tile:
                    weights = [jnp.where(line >= 4, weight, 0.0) for weight in weights]
                base = jnp.where(inside, 0.0, main[j]) if job["inverse"] else main[j]
                z = solved[0]
                main[j] = base - (
                    (weights[0] * z[0] + weights[1] * z[1]) + (weights[2] * z[2] + weights[3] * z[3])
                )
                if extra:
                    z = solved[1]
                    extra[j] = extra[j] - (
                        (weights[0] * z[0] + weights[1] * z[1]) + (weights[2] * z[2] + weights[3] * z[3])
                    )
    row = lax.broadcasted_iota(jnp.int32, (HALF, HALF), 0)
    col = lax.broadcasted_iota(jnp.int32, (HALF, HALF), 1)
    results = []
    for job, (done_main, done_extra) in zip(jobs, done):
        main = jnp.concatenate(done_main, 0)
        keep = (col <= row) if job["inverse"] else (col >= row)
        main = jnp.where(keep, main, 0.0)
        results.append((main, jnp.concatenate(done_extra, 0) if job["extra"] else None))
    return results


def tiles_of(matrix):
    return [matrix[8 * i : 8 * i + 8, :] for i in range(HALF // 8)]


def factors(packed_ref, pivot_ref, weights_ref, offset_ref, factor_ref):
    channels = 2 * HALF
    base = 4 * HALF
    line0 = packed_ref[base : base + 8, :]
    number = jnp.broadcast_to(line0[2:3, 0:1], (1, HALF))
    pairs = jnp.broadcast_to(line0[3:4, 0:1], (1, HALF))
    noise_scale = 1.0 / (2.0 * pairs)
    scale = 1.0 / number
    mean0, mean1 = line0[0:1] * scale, line0[1:2] * scale
    column0 = as_column(mean0)
    column1 = as_column(mean1)
    part = lambda i: packed_ref[HALF * i : HALF * (i + 1), :]
    row = lax.broadcasted_iota(jnp.int32, (HALF, HALF), 0)
    col = lax.broadcasted_iota(jnp.int32, (HALF, HALF), 1)

    def diagonal_blocks(block, diagonal):
        turned = jnp.transpose(block)
        lower = jnp.where(col <= row, block, turned)
        upper = jnp.where(col > row, block, turned)
        return lower, jnp.where(col == row, diagonal, upper)

    n00, n11 = (block * noise_scale for block in diagonal_blocks(part(0), line0[4:5]))
    n01 = part(1) * noise_scale
    s00, s11 = diagonal_blocks(part(2), line0[5:6])
    s00 = s00 * scale - column0 * mean0
    s01 = part(3) * scale - column0 * mean1
    s11 = s11 * scale - column1 * mean1
    (w00, y), (k00, k01) = eliminate(
        [
            dict(main=tiles_of(n00), extra=tiles_of(n01), inverse=True),
            dict(main=tiles_of(s00), extra=tiles_of(s01), inverse=False),
        ]
    )
    n11 = n11 - exact(y, y, 0, 0)
    s11 = s11 - exact(k01, k01, 0, 0)
    (w11, _), (k11, _) = eliminate(
        [
            dict(main=tiles_of(n11), extra=None, inverse=True),
            dict(main=tiles_of(s11), extra=None, inverse=False),
        ]
    )
    w10 = -exact(w11, exact(y, w00, 0, 0))
    factor_ref[:HALF, :HALF] = exact(k00, w00, 1, 1)
    factor_ref[:HALF, HALF:] = exact(k00, w10, 1, 1) + exact(k01, w11, 1, 1)
    factor_ref[HALF:, :HALF] = jnp.zeros((HALF, HALF), F32)
    factor_ref[HALF:, HALF:] = exact(k11, w11, 1, 1)
    mean0 = jnp.broadcast_to(mean0, (8, HALF)) - pivot_ref[:, :HALF]
    mean1 = jnp.broadcast_to(mean1, (8, HALF)) - pivot_ref[:, HALF:]
    offset_ref[:, :HALF] = exact(mean0, w00, 1, 1)
    offset_ref[:, HALF:] = exact(mean0, w10, 1, 1) + exact(mean1, w11, 1, 1)
    left = jnp.concatenate([jnp.transpose(w00), jnp.zeros((HALF, HALF), F32)], 0)
    right = jnp.concatenate([jnp.transpose(w10), jnp.transpose(w11)], 0)
    high, low = split(jnp.concatenate([left, right], 1))
    weights_ref[0:channels, :] = high
    weights_ref[channels : 2 * channels, :] = low
    weights_ref[2 * channels :, :] = high


def whiten_rows(high, low, weights):
    return jnp.dot(jnp.concatenate([high, high, low], 1), weights, preferred_element_type=F32)


def whiten_kernel(
    packed_ref,
    pivot_ref,
    high_from,
    low_from,
    valid_ref,
    below_ref,
    right_ref,
    white_ref,
    noise_ref,
    factor_ref,
    high_ref,
    low_ref,
    weights_ref,
    offset_ref,
    plain,
    right_edge,
    neighbours,
    arrived,
):
    step = pl.program_id(0)
    steps = pl.num_programs(0)
    rows, cols = valid_ref.shape
    channels = high_ref.shape[2]

    @pl.when(step == 0)
    def _():
        valid = valid_ref[...].astype(F32)
        down = jnp.concatenate([valid[1:], below_ref[cols : cols + 1, :]], 0)
        right = jnp.concatenate([valid[:, 1:], right_ref[:, channels : channels + 1]], 1)
        neighbours[...] = down + right
        copies = [
            pltpu.make_async_copy(high_from, high_ref, arrived.at[0]),
            pltpu.make_async_copy(low_from, low_ref, arrived.at[1]),
        ]
        for copy in copies:
            copy.start()
        factors(packed_ref, pivot_ref, weights_ref, offset_ref, factor_ref)
        pivot = pivot_ref[0:1, :]
        below = below_ref[0:cols, :] - as_column(below_ref[cols : cols + 1, :]) * pivot
        plain[STEP_ROWS * (cols + 8) :, :] = whiten_rows(*split(below), weights_ref[...])
        right = right_ref[:, :channels] - right_ref[:, channels : channels + 1] * pivot
        right_edge[...] = whiten_rows(*split(right), weights_ref[...])
        for copy in copies:
            copy.wait()

    start = pl.multiple_of((steps - 1 - step) * STEP_ROWS, STEP_ROWS)
    valid = jnp.transpose(valid_ref[pl.ds(start, STEP_ROWS), :].astype(F32))
    number = jnp.transpose(neighbours[pl.ds(start, STEP_ROWS), :])
    edge = right_edge[pl.ds(start, STEP_ROWS), :]
    offset = offset_ref[0:1, :]
    weights = weights_ref[...]
    for row in reversed(range(STEP_ROWS)):
        base = row * (cols + 8)
        plain[base : base + cols, :] = whiten_rows(high_ref[start + row], low_ref[start + row], weights)
        plain[base + cols : base + cols + 1, :] = edge[row : row + 1]
        for at in range(0, cols, CHUNK):
            here = plain[base + at : base + at + CHUNK, :]
            right = plain[base + at + 1 : base + at + 1 + CHUNK, :]
            below = plain[base + cols + 8 + at : base + cols + 8 + at + CHUNK, :]
            ok = valid[at : at + CHUNK, row : row + 1]
            white_ref[row, at : at + CHUNK, :] = (here - ok * offset).astype(BF16)
            around = number[at : at + CHUNK, row : row + 1]
            noise_ref[row, at : at + CHUNK, :] = (ok * (below + right) - around * here).astype(BF16)
    plain[STEP_ROWS * (cols + 8) :, :] = plain[0 : cols, :]


def whiten(packed, pivot, high, low, good_pixels, below, right):
    rows, cols, channels = high.shape
    steps = rows // STEP_ROWS
    pixels = rows * cols
    whole = lambda shape: pl.BlockSpec(shape, lambda i: (0,) * len(shape))
    block = pl.BlockSpec((STEP_ROWS, cols, channels), lambda i: (steps - 1 - i, 0, 0))
    return pl.pallas_call(
        whiten_kernel,
        grid=(steps,),
        in_specs=[
            whole(packed.shape),
            whole(pivot.shape),
            pl.BlockSpec(memory_space=pl.ANY),
            pl.BlockSpec(memory_space=pl.ANY),
            whole((rows, cols)),
            whole(below.shape),
            whole(right.shape),
        ],
        out_specs=[block, block, whole((channels, channels))],
        out_shape=[jax.ShapeDtypeStruct(high.shape, BF16)] * 2 + [jax.ShapeDtypeStruct((channels, channels), F32)],
        scratch_shapes=[
            pltpu.VMEM(high.shape, BF16),
            pltpu.VMEM(low.shape, BF16),
            pltpu.VMEM((3 * channels, channels), BF16),
            pltpu.VMEM((8, channels), F32),
            pltpu.VMEM((STEP_ROWS * (cols + 8) + cols, channels), F32),
            pltpu.VMEM((rows, channels), F32),
            pltpu.VMEM((rows, cols), F32),
            pltpu.SemaphoreType.DMA((2,)),
        ],
        compiler_params=pltpu.CompilerParams(vmem_limit_bytes=48 * 1024 * 1024),
        cost_estimate=pl.CostEstimate(
            flops=6 * pixels * channels * channels, bytes_accessed=8 * pixels * channels, transcendentals=0
        ),
        name="whiten",
    )(packed, pivot, high, low, good_pixels, below, right)


def from_next(value, axis):
    count = lax.axis_size(axis)
    return lax.ppermute(value, axis, [(source, source - 1) for source in range(1, count)])


def summed(packed):
    axes = ("col", "row")
    cols, rows = (lax.axis_size(axis) for axis in axes)
    core = lax.axis_index("row") % 2
    swap = [(i, i ^ 1) for i in range(rows)]
    groups = [[c * rows + r for c in range(cols) for r in range(k, rows, 2)] for k in range(2)]
    peers = cols * rows // 2
    parts = packed.reshape(2, packed.shape[0] // 2, HALF)
    kept = lax.dynamic_index_in_dim(parts, core, 0, keepdims=False)
    given = lax.dynamic_index_in_dim(parts, 1 - core, 0, keepdims=False)
    share = (kept + lax.ppermute(given, "row", swap)).reshape(peers, -1, 1, HALF)
    mine = jnp.sum(lax.all_to_all(share, axes, 0, 0, axis_index_groups=groups), 0)
    every = lax.all_to_all(jnp.broadcast_to(mine[None], share.shape), axes, 0, 0, axis_index_groups=groups)
    every = every.reshape(kept.shape)
    other = lax.ppermute(every, "row", swap)
    return jnp.concatenate([jnp.where(core == 0, every, other), jnp.where(core == 0, other, every)], 0)


def on_device(raw_counts, gain_class, good_pixels, class_gains):
    raw_counts = pltpu.with_memory_space_constraint(raw_counts, pltpu.HBM)
    first_row, first_col = edges(raw_counts, gain_class, good_pixels, class_gains)
    below = from_next(first_row, "row")
    right = from_next(first_col, "col")
    high, low, products, sums, pivot = moments(raw_counts, gain_class, good_pixels, class_gains)
    high, low = (pltpu.with_memory_space_constraint(part, pltpu.HBM) for part in (high, low))
    devices = lax.axis_size(("col", "row"))
    length = -(-(4 * HALF + 8) // devices) * devices
    packed = pack(products, sums, pivot, below, right, high, low, good_pixels, length)
    return whiten(summed(packed), pivot, high, low, good_pixels, below, right)


def solution(mesh):
    return jax.shard_map(
        on_device,
        mesh=mesh,
        in_specs=(P("row", "col", None), P("row", "col"), P("row", "col"), P()),
        out_specs=(P("row", "col", None), P("row", "col", None), P()),
        check_vma=False,
    )
```

```python
import jax
import jax.numpy as jnp
from jax import lax
from jax.experimental import pallas as pl
from jax.experimental.pallas import tpu as pltpu
from jax.sharding import PartitionSpec as P

STEP_ROWS = 16
CHUNK = 32
HALF = 128
HIGHEST = lax.Precision.HIGHEST
F32 = jnp.float32
BF16 = jnp.bfloat16


def over_pixels(left, right):
    return lax.dot_general(left, right, (((0,), (0,)), ((), ())), preferred_element_type=F32)


def exact(left, right, left_dim=1, right_dim=0):
    return lax.dot_general(
        left,
        right,
        (((left_dim,), (right_dim,)), ((), ())),
        precision=HIGHEST,
        preferred_element_type=F32,
    )


def split(value):
    high = value.astype(BF16)
    return high, (value - high.astype(F32)).astype(BF16)


def stacked_gains(gains):
    high = gains.astype(BF16)
    rest = gains - high.astype(F32)
    middle = rest.astype(BF16)
    low = (rest - middle.astype(F32)).astype(BF16)
    return jnp.concatenate([high, middle, low], 0)


def row_gains(classes, valid, gains, count):
    which = lax.rem(lax.broadcasted_iota(jnp.int32, (3 * count, classes.shape[1]), 0), count)
    onehot = jnp.where((which == classes) & (valid > 0), 1.0, 0.0).astype(BF16)
    return over_pixels(onehot, gains)


def as_column(row):
    return jnp.transpose(jnp.broadcast_to(row, (8, row.shape[1])))[:, :1]


def edges_kernel(row_ref, col_ref, class_ref, valid_ref, gains_ref, row_out, col_out):
    count = gains_ref.shape[0]
    gains = stacked_gains(gains_ref[...])
    cols = row_ref.shape[1]
    rows = col_ref.shape[0]
    calibrated = row_ref[0].astype(F32) * row_gains(class_ref[0:1, :], valid_ref[0:1, :], gains, count)
    row_out[0:cols, :] = calibrated
    row_out[cols:, :] = jnp.broadcast_to(valid_ref[0:1, :].astype(F32), (8, cols))
    which = lax.rem(lax.broadcasted_iota(jnp.int32, (rows, 3 * count), 1), count)
    first_valid = valid_ref[:, 0:1]
    onehot = jnp.where((which == class_ref[:, 0:1]) & (first_valid > 0), 1.0, 0.0).astype(BF16)
    gain_col = jnp.dot(onehot, gains, preferred_element_type=F32)
    channels = gain_col.shape[1]
    raw_col = col_ref[...].astype(F32)[:, 0, :]
    col_out[:, :channels] = raw_col * gain_col
    col_out[:, channels:] = jnp.broadcast_to(first_valid.astype(F32), (rows, 128))


def edges(raw_counts, gain_class, good_pixels, class_gains):
    rows, cols, channels = raw_counts.shape
    whole = lambda shape: pl.BlockSpec(shape, lambda i: (0,) * len(shape))
    return pl.pallas_call(
        edges_kernel,
        grid=(1,),
        in_specs=[
            whole((1, cols, channels)),
            whole((rows, 16, channels)),
            whole((rows, cols)),
            whole((rows, cols)),
            whole(class_gains.shape),
        ],
        out_specs=[whole((cols + 8, channels)), whole((rows, channels + 128))],
        out_shape=[
            jax.ShapeDtypeStruct((cols + 8, channels), F32),
            jax.ShapeDtypeStruct((rows, channels + 128), F32),
        ],
        name="edges",
    )(raw_counts, raw_counts, gain_class, good_pixels, class_gains)


def moments_kernel(
    raw_ref, class_ref, valid_ref, gains_ref, high_ref, low_ref, products_ref, sums_ref, pivot_ref, last_row_ref, last_col_ref, plain, half_degree, terms, gains_bf
):
    step = pl.program_id(0)
    count = gains_ref.shape[0]
    rows, cols = valid_ref.shape
    channels = raw_ref.shape[2]

    @pl.when(step == 0)
    def _():
        valid = valid_ref[...].astype(F32)
        zero_row = jnp.zeros((1, cols), F32)
        zero_col = jnp.zeros((rows, 1), F32)
        degree = jnp.concatenate([valid[1:], zero_row], 0) + jnp.concatenate([zero_row, valid[:-1]], 0)
        degree = degree + jnp.concatenate([valid[:, 1:], zero_col], 1) + jnp.concatenate([zero_col, valid[:, :-1]], 1)
        half_degree[...] = 0.5 * degree
        plain[...] = jnp.zeros_like(plain)
        products_ref[...] = jnp.zeros_like(products_ref)
        sums_ref[...] = jnp.zeros_like(sums_ref)
        gains_bf[...] = stacked_gains(gains_ref[...])
        gain_map = row_gains(class_ref[0:1, :], valid_ref[0:1, :], gains_bf[...], count)
        number = jnp.maximum(jnp.sum(valid[0:1, :], keepdims=True), 1.0)
        pivot = jnp.sum(raw_ref[0].astype(F32) * gain_map, 0, keepdims=True) / number
        pivot_ref[...] = jnp.broadcast_to(pivot, pivot_ref.shape)

    start = pl.multiple_of(step * STEP_ROWS, STEP_ROWS)
    classes = class_ref[pl.ds(start, STEP_ROWS), :]
    valid = valid_ref[pl.ds(start, STEP_ROWS), :]
    degrees = jnp.transpose(half_degree[pl.ds(start, STEP_ROWS), :])
    valid_cols = jnp.transpose(valid.astype(F32))
    pivot = pivot_ref[0:1, :]
    gains = gains_bf[...]
    total = sums_ref[...]
    for row in range(STEP_ROWS):
        gain_map = row_gains(classes[row : row + 1], valid[row : row + 1], gains, count)
        for at in range(0, cols, CHUNK):
            calibrated = raw_ref[row, at : at + CHUNK, :].astype(F32) * gain_map[at : at + CHUNK]
            calibrated = calibrated - valid_cols[at : at + CHUNK, row : row + 1] * pivot
            high, low = split(calibrated)
            high_ref[row, at : at + CHUNK, :] = high
            low_ref[row, at : at + CHUNK, :] = low
            plain[row % 2, 8 + at : 8 + at + CHUNK, :] = calibrated
            left = plain[row % 2, 7 + at : 7 + at + CHUNK, :]
            above = plain[1 - row % 2, 8 + at : 8 + at + CHUNK, :]
            term = above + left - degrees[at : at + CHUNK, row : row + 1] * calibrated
            terms[row * cols + at : row * cols + at + CHUNK, :] = term.astype(BF16)
            total = total + jnp.sum(calibrated.reshape(CHUNK // 8, 8, channels), 0)
        last_col_ref[pl.ds(start + row, 1), :] = calibrated[CHUNK - 1 :, :]
    sums_ref[...] = total
    last_row_ref[...] = plain[(STEP_ROWS - 1) % 2, 8:, :]
    pixels = STEP_ROWS * cols
    high = high_ref[...].reshape(pixels, channels)
    products_ref[...] += over_pixels(high, jnp.concatenate([terms[...], high], 1))


def moments(raw_counts, gain_class, good_pixels, class_gains):
    rows, cols, channels = raw_counts.shape
    whole = lambda shape: pl.BlockSpec(shape, lambda i: (0,) * len(shape))
    block = pl.BlockSpec((STEP_ROWS, cols, channels), lambda i: (i, 0, 0))
    pixels = rows * cols
    return pl.pallas_call(
        moments_kernel,
        grid=(rows // STEP_ROWS,),
        in_specs=[block, whole((rows, cols)), whole((rows, cols)), whole(class_gains.shape)],
        out_specs=[block, block, whole((channels, 2 * channels)), whole((8, channels)), whole((8, channels)), whole((cols, channels)), whole((rows, channels))],
        out_shape=[
            pltpu.HBM(raw_counts.shape, BF16),
            pltpu.HBM(raw_counts.shape, BF16),
            jax.ShapeDtypeStruct((channels, 2 * channels), F32),
            jax.ShapeDtypeStruct((8, channels), F32),
            jax.ShapeDtypeStruct((8, channels), F32),
            jax.ShapeDtypeStruct((cols, channels), F32),
            jax.ShapeDtypeStruct((rows, channels), F32),
        ],
        scratch_shapes=[
            pltpu.VMEM((2, 8 + cols, channels), F32),
            pltpu.VMEM((rows, cols), F32),
            pltpu.VMEM((STEP_ROWS * cols, channels), BF16),
            pltpu.VMEM((3 * class_gains.shape[0], channels), BF16),
        ],
        compiler_params=pltpu.CompilerParams(vmem_limit_bytes=32 * 1024 * 1024),
        cost_estimate=pl.CostEstimate(
            flops=10 * pixels * channels * channels, bytes_accessed=6 * pixels * channels, transcendentals=0
        ),
        name="moments",
    )(raw_counts, gain_class, good_pixels, class_gains)


def pack_kernel(
    products_ref, sums_ref, pivot_ref, below_ref, right_ref, last_row_ref, last_col_ref, valid_ref, packed_ref
):
    rows, cols = valid_ref.shape
    channels = sums_ref.shape[1]
    valid = valid_ref[...].astype(F32)
    last_valid = as_column(valid[rows - 1 : rows, :])
    below_row = below_ref[cols : cols + 1, :]
    below_valid = as_column(below_row)
    mine = last_row_ref[...]
    pivot = pivot_ref[0:1, :]
    down = last_valid * (below_ref[0:cols, :] - below_valid * pivot) - below_valid * mine
    right_valid = right_ref[:, channels : channels + 1]
    mine = last_col_ref[...]
    last_col = valid[:, cols - 1 : cols]
    right = last_col * (right_ref[:, :channels] - right_valid * pivot) - right_valid * mine
    edge = jnp.concatenate([down, right], 0).astype(BF16)
    cross = products_ref[:, :channels]
    noise = over_pixels(edge, edge) - (cross + jnp.transpose(cross))
    number = jnp.sum(valid, keepdims=True)
    total = jnp.sum(sums_ref[...], 0, keepdims=True)
    shift = total + number * pivot
    second = products_ref[:, channels:] + (as_column(pivot) * shift + as_column(total) * pivot)
    total = shift
    row = lax.broadcasted_iota(jnp.int32, (HALF, HALF), 0)
    col = lax.broadcasted_iota(jnp.int32, (HALF, HALF), 1)
    at = 0
    diagonals = []
    for matrix in (noise, second):
        packed_ref[at : at + HALF, :] = jnp.where(col <= row, matrix[:HALF, :HALF], matrix[HALF:, HALF:])
        packed_ref[at + HALF : at + 2 * HALF, :] = matrix[:HALF, HALF:]
        diagonals.append(jnp.sum(jnp.where(row == col, matrix[HALF:, HALF:], 0.0), 0, keepdims=True))
        at += 2 * HALF
    pairs = jnp.sum(valid[1:] * valid[:-1], keepdims=True) + jnp.sum(valid[:, 1:] * valid[:, :-1], keepdims=True)
    pairs = pairs + jnp.sum(valid[rows - 1 :] * below_row, keepdims=True)
    pairs = pairs + jnp.sum(last_col * right_valid, keepdims=True)
    line = lax.broadcasted_iota(jnp.int32, (8, HALF), 0)
    packed_ref[at : at + 8, :] = jnp.where(
        line == 0,
        total[:, :HALF],
        jnp.where(
            line == 1,
            total[:, HALF:],
            jnp.where(
                line == 2,
                number,
                jnp.where(
                    line == 3, pairs, jnp.where(line == 4, diagonals[0], jnp.where(line == 5, diagonals[1], 0.0))
                ),
            ),
        ),
    )
    if packed_ref.shape[0] > at + 8:
        packed_ref[at + 8 :, :] = jnp.zeros((packed_ref.shape[0] - at - 8, HALF), F32)


def pack(products, sums, pivot, below, right, last_row, last_col, good_pixels, length):
    rows, cols = good_pixels.shape
    whole = lambda shape: pl.BlockSpec(shape, lambda i: (0,) * len(shape))
    return pl.pallas_call(
        pack_kernel,
        grid=(1,),
        in_specs=[
            whole(products.shape),
            whole(sums.shape),
            whole(pivot.shape),
            whole(below.shape),
            whole(right.shape),
            whole(last_row.shape),
            whole(last_col.shape),
            whole((rows, cols)),
        ],
        out_specs=whole((length, HALF)),
        out_shape=jax.ShapeDtypeStruct((length, HALF), F32),
        compiler_params=pltpu.CompilerParams(vmem_limit_bytes=32 * 1024 * 1024),
        name="pack",
    )(products, sums, pivot, below, right, last_row, last_col, good_pixels)


def inverse_of_pair(a, b, c):
    scale = 1.0 / (a * c - b * b)
    return c * scale, -(b * scale), a * scale


def eliminate(jobs):
    lane = lax.broadcasted_iota(jnp.int32, (8, HALF), 1)
    line = lax.broadcasted_iota(jnp.int32, (8, HALF), 0)
    spread = lambda value: jnp.broadcast_to(value, (8, HALF))
    pick = lambda value, place: jnp.take_along_axis(
        value, jnp.full((8, HALF), place, jnp.int32), axis=1, mode="promise_in_bounds"
    )
    tiles = HALF // 8
    done = [([None] * tiles, [None] * tiles) for _ in jobs]
    for turn in range(HALF // 4):
        tile, first, at = turn // 2, 4 * (turn % 2), 4 * turn
        for job, (done_main, done_extra) in zip(jobs, done):
            main, extra = job["main"], job["extra"]
            lead = main[tile]
            rows = [spread(lead[first + i : first + i + 1, :]) for i in range(4)]
            p = {(i, j): pick(rows[i], at + j) for i in range(4) for j in range(i, 4)}
            if job["inverse"]:
                inside = (lane >= at) & (lane < at + 4)
                rows = [jnp.where(inside, jnp.where(lane == at + i, 1.0, 0.0), row) for i, row in enumerate(rows)]
            more = [spread(extra[tile][first + i : first + i + 1, :]) for i in range(4)] if extra else None
            e00, e01, e11 = inverse_of_pair(p[0, 0], p[0, 1], p[1, 1])
            f00 = e00 * p[0, 2] + e01 * p[1, 2]
            f10 = e01 * p[0, 2] + e11 * p[1, 2]
            f01 = e00 * p[0, 3] + e01 * p[1, 3]
            f11 = e01 * p[0, 3] + e11 * p[1, 3]
            g00, g01, g11 = inverse_of_pair(
                p[2, 2] - (p[0, 2] * f00 + p[1, 2] * f10),
                p[2, 3] - (p[0, 2] * f01 + p[1, 2] * f11),
                p[3, 3] - (p[0, 3] * f01 + p[1, 3] * f11),
            )
            i0 = lax.rsqrt(p[0, 0])
            l10, l20, l30 = p[0, 1] * i0, p[0, 2] * i0, p[0, 3] * i0
            i1 = lax.rsqrt(p[1, 1] - l10 * l10)
            l21, l31 = (p[1, 2] - l20 * l10) * i1, (p[1, 3] - l30 * l10) * i1
            i2 = lax.rsqrt(p[2, 2] - (l20 * l20 + l21 * l21))
            l32 = (p[2, 3] - (l30 * l20 + l31 * l21)) * i2
            i3 = lax.rsqrt(p[3, 3] - (l30 * l30 + l31 * l31 + l32 * l32))
            solved = []
            for group, target in ((rows, done_main), (more, done_extra)):
                if group is None:
                    solved.append(None)
                    continue
                u2 = group[2] - (f00 * group[0] + f10 * group[1])
                u3 = group[3] - (f01 * group[0] + f11 * group[1])
                z2 = g00 * u2 + g01 * u3
                z3 = g01 * u2 + g11 * u3
                z0 = (e00 * group[0] + e01 * group[1]) - (f00 * z2 + f01 * z3)
                z1 = (e01 * group[0] + e11 * group[1]) - (f10 * z2 + f11 * z3)
                solved.append((z0, z1, z2, z3))
                r0 = group[0] * i0
                r1 = (group[1] - l10 * r0) * i1
                r2 = (group[2] - (l20 * r0 + l21 * r1)) * i2
                r3 = (group[3] - (l30 * r0 + l31 * r1 + l32 * r2)) * i3
                quad = jnp.where(
                    line == first,
                    r0,
                    jnp.where(line == first + 1, r1, jnp.where(line == first + 2, r2, r3)),
                )
                target[tile] = quad if first == 0 else jnp.where(line < 4, target[tile], quad)
            for j in range(tile if first == 0 else tile + 1, tiles):
                weights = [spread(main[j][:, at + i : at + i + 1]) for i in range(4)]
                if j == tile:
                    weights = [jnp.where(line >= 4, weight, 0.0) for weight in weights]
                base = jnp.where(inside, 0.0, main[j]) if job["inverse"] else main[j]
                z = solved[0]
                main[j] = base - (
                    (weights[0] * z[0] + weights[1] * z[1]) + (weights[2] * z[2] + weights[3] * z[3])
                )
                if extra:
                    z = solved[1]
                    extra[j] = extra[j] - (
                        (weights[0] * z[0] + weights[1] * z[1]) + (weights[2] * z[2] + weights[3] * z[3])
                    )
    row = lax.broadcasted_iota(jnp.int32, (HALF, HALF), 0)
    col = lax.broadcasted_iota(jnp.int32, (HALF, HALF), 1)
    results = []
    for job, (done_main, done_extra) in zip(jobs, done):
        main = jnp.concatenate(done_main, 0)
        keep = (col <= row) if job["inverse"] else (col >= row)
        main = jnp.where(keep, main, 0.0)
        results.append((main, jnp.concatenate(done_extra, 0) if job["extra"] else None))
    return results


def tiles_of(matrix):
    return [matrix[8 * i : 8 * i + 8, :] for i in range(HALF // 8)]


def factors(packed_ref, pivot_ref, weights_ref, offset_ref, factor_ref):
    channels = 2 * HALF
    base = 4 * HALF
    line0 = packed_ref[base : base + 8, :]
    number = jnp.broadcast_to(line0[2:3, 0:1], (1, HALF))
    pairs = jnp.broadcast_to(line0[3:4, 0:1], (1, HALF))
    noise_scale = 1.0 / (2.0 * pairs)
    scale = 1.0 / number
    mean0, mean1 = line0[0:1] * scale, line0[1:2] * scale
    column0 = as_column(mean0)
    column1 = as_column(mean1)
    part = lambda i: packed_ref[HALF * i : HALF * (i + 1), :]
    row = lax.broadcasted_iota(jnp.int32, (HALF, HALF), 0)
    col = lax.broadcasted_iota(jnp.int32, (HALF, HALF), 1)

    def diagonal_blocks(block, diagonal):
        turned = jnp.transpose(block)
        lower = jnp.where(col <= row, block, turned)
        upper = jnp.where(col > row, block, turned)
        return lower, jnp.where(col == row, diagonal, upper)

    n00, n11 = (block * noise_scale for block in diagonal_blocks(part(0), line0[4:5]))
    n01 = part(1) * noise_scale
    s00, s11 = diagonal_blocks(part(2), line0[5:6])
    s00 = s00 * scale - column0 * mean0
    s01 = part(3) * scale - column0 * mean1
    s11 = s11 * scale - column1 * mean1
    (w00, y), (k00, k01) = eliminate(
        [
            dict(main=tiles_of(n00), extra=tiles_of(n01), inverse=True),
            dict(main=tiles_of(s00), extra=tiles_of(s01), inverse=False),
        ]
    )
    n11 = n11 - exact(y, y, 0, 0)
    s11 = s11 - exact(k01, k01, 0, 0)
    (w11, _), (k11, _) = eliminate(
        [
            dict(main=tiles_of(n11), extra=None, inverse=True),
            dict(main=tiles_of(s11), extra=None, inverse=False),
        ]
    )
    w10 = -exact(w11, exact(y, w00, 0, 0))
    factor_ref[:HALF, :HALF] = exact(k00, w00, 1, 1)
    factor_ref[:HALF, HALF:] = exact(k00, w10, 1, 1) + exact(k01, w11, 1, 1)
    factor_ref[HALF:, :HALF] = jnp.zeros((HALF, HALF), F32)
    factor_ref[HALF:, HALF:] = exact(k11, w11, 1, 1)
    mean0 = jnp.broadcast_to(mean0, (8, HALF)) - pivot_ref[:, :HALF]
    mean1 = jnp.broadcast_to(mean1, (8, HALF)) - pivot_ref[:, HALF:]
    offset_ref[:, :HALF] = exact(mean0, w00, 1, 1)
    offset_ref[:, HALF:] = exact(mean0, w10, 1, 1) + exact(mean1, w11, 1, 1)
    left = jnp.concatenate([jnp.transpose(w00), jnp.zeros((HALF, HALF), F32)], 0)
    right = jnp.concatenate([jnp.transpose(w10), jnp.transpose(w11)], 0)
    high, low = split(jnp.concatenate([left, right], 1))
    weights_ref[0:channels, :] = high
    weights_ref[channels : 2 * channels, :] = low
    weights_ref[2 * channels :, :] = high


def whiten_rows(high, low, weights):
    return jnp.dot(jnp.concatenate([high, high, low], 1), weights, preferred_element_type=F32)


def whiten_kernel(
    packed_ref,
    pivot_ref,
    high_from,
    low_from,
    valid_ref,
    below_ref,
    right_ref,
    white_ref,
    noise_ref,
    factor_ref,
    high_ref,
    low_ref,
    weights_ref,
    offset_ref,
    plain,
    right_edge,
    neighbours,
    arrived,
):
    step = pl.program_id(0)
    steps = pl.num_programs(0)
    rows, cols = valid_ref.shape
    channels = high_ref.shape[2]

    @pl.when(step == 0)
    def _():
        valid = valid_ref[...].astype(F32)
        down = jnp.concatenate([valid[1:], below_ref[cols : cols + 1, :]], 0)
        right = jnp.concatenate([valid[:, 1:], right_ref[:, channels : channels + 1]], 1)
        neighbours[...] = down + right
        copies = [
            pltpu.make_async_copy(high_from, high_ref, arrived.at[0]),
            pltpu.make_async_copy(low_from, low_ref, arrived.at[1]),
        ]
        for copy in copies:
            copy.start()
        factors(packed_ref, pivot_ref, weights_ref, offset_ref, factor_ref)
        pivot = pivot_ref[0:1, :]
        below = below_ref[0:cols, :] - as_column(below_ref[cols : cols + 1, :]) * pivot
        plain[STEP_ROWS * (cols + 8) :, :] = whiten_rows(*split(below), weights_ref[...])
        right = right_ref[:, :channels] - right_ref[:, channels : channels + 1] * pivot
        right_edge[...] = whiten_rows(*split(right), weights_ref[...])
        for copy in copies:
            copy.wait()

    start = pl.multiple_of((steps - 1 - step) * STEP_ROWS, STEP_ROWS)
    valid = jnp.transpose(valid_ref[pl.ds(start, STEP_ROWS), :].astype(F32))
    number = jnp.transpose(neighbours[pl.ds(start, STEP_ROWS), :])
    edge = right_edge[pl.ds(start, STEP_ROWS), :]
    offset = offset_ref[0:1, :]
    weights = weights_ref[...]
    for row in reversed(range(STEP_ROWS)):
        base = row * (cols + 8)
        plain[base : base + cols, :] = whiten_rows(high_ref[start + row], low_ref[start + row], weights)
        plain[base + cols : base + cols + 1, :] = edge[row : row + 1]
        for at in range(0, cols, CHUNK):
            here = plain[base + at : base + at + CHUNK, :]
            right = plain[base + at + 1 : base + at + 1 + CHUNK, :]
            below = plain[base + cols + 8 + at : base + cols + 8 + at + CHUNK, :]
            ok = valid[at : at + CHUNK, row : row + 1]
            white_ref[row, at : at + CHUNK, :] = (here - ok * offset).astype(BF16)
            around = number[at : at + CHUNK, row : row + 1]
            noise_ref[row, at : at + CHUNK, :] = (ok * (below + right) - around * here).astype(BF16)
    plain[STEP_ROWS * (cols + 8) :, :] = plain[0 : cols, :]


def whiten(packed, pivot, high, low, good_pixels, below, right):
    rows, cols, channels = high.shape
    steps = rows // STEP_ROWS
    pixels = rows * cols
    whole = lambda shape: pl.BlockSpec(shape, lambda i: (0,) * len(shape))
    block = pl.BlockSpec((STEP_ROWS, cols, channels), lambda i: (steps - 1 - i, 0, 0))
    return pl.pallas_call(
        whiten_kernel,
        grid=(steps,),
        in_specs=[
            whole(packed.shape),
            whole(pivot.shape),
            pl.BlockSpec(memory_space=pl.ANY),
            pl.BlockSpec(memory_space=pl.ANY),
            whole((rows, cols)),
            whole(below.shape),
            whole(right.shape),
        ],
        out_specs=[block, block, whole((channels, channels))],
        out_shape=[jax.ShapeDtypeStruct(high.shape, BF16)] * 2 + [jax.ShapeDtypeStruct((channels, channels), F32)],
        scratch_shapes=[
            pltpu.VMEM(high.shape, BF16),
            pltpu.VMEM(low.shape, BF16),
            pltpu.VMEM((3 * channels, channels), BF16),
            pltpu.VMEM((8, channels), F32),
            pltpu.VMEM((STEP_ROWS * (cols + 8) + cols, channels), F32),
            pltpu.VMEM((rows, channels), F32),
            pltpu.VMEM((rows, cols), F32),
            pltpu.SemaphoreType.DMA((2,)),
        ],
        compiler_params=pltpu.CompilerParams(vmem_limit_bytes=48 * 1024 * 1024),
        cost_estimate=pl.CostEstimate(
            flops=6 * pixels * channels * channels, bytes_accessed=8 * pixels * channels, transcendentals=0
        ),
        name="whiten",
    )(packed, pivot, high, low, good_pixels, below, right)


def from_next(value, axis):
    count = lax.axis_size(axis)
    return lax.ppermute(value, axis, [(source, source - 1) for source in range(1, count)])


def summed(packed):
    axes = ("col", "row")
    cols, rows = (lax.axis_size(axis) for axis in axes)
    core = lax.axis_index("row") % 2
    swap = [(i, i ^ 1) for i in range(rows)]
    groups = [[c * rows + r for c in range(cols) for r in range(k, rows, 2)] for k in range(2)]
    peers = cols * rows // 2
    parts = packed.reshape(2, packed.shape[0] // 2, HALF)
    kept = lax.dynamic_index_in_dim(parts, core, 0, keepdims=False)
    given = lax.dynamic_index_in_dim(parts, 1 - core, 0, keepdims=False)
    share = (kept + lax.ppermute(given, "row", swap)).reshape(peers, -1, 1, HALF)
    mine = jnp.sum(lax.all_to_all(share, axes, 0, 0, axis_index_groups=groups), 0)
    every = lax.all_to_all(jnp.broadcast_to(mine[None], share.shape), axes, 0, 0, axis_index_groups=groups)
    every = every.reshape(kept.shape)
    other = lax.ppermute(every, "row", swap)
    return jnp.concatenate([jnp.where(core == 0, every, other), jnp.where(core == 0, other, every)], 0)


def on_device(raw_counts, gain_class, good_pixels, class_gains):
    raw_counts = pltpu.with_memory_space_constraint(raw_counts, pltpu.HBM)
    first_row, first_col = edges(raw_counts, gain_class, good_pixels, class_gains)
    below = from_next(first_row, "row")
    right = from_next(first_col, "col")
    high, low, products, sums, pivot, last_row, last_col = moments(raw_counts, gain_class, good_pixels, class_gains)
    high, low = (pltpu.with_memory_space_constraint(part, pltpu.HBM) for part in (high, low))
    devices = lax.axis_size(("col", "row"))
    length = -(-(4 * HALF + 8) // devices) * devices
    packed = pack(products, sums, pivot, below, right, last_row, last_col, good_pixels, length)
    return whiten(summed(packed), pivot, high, low, good_pixels, below, right)


def solution(mesh):
    return jax.shard_map(
        on_device,
        mesh=mesh,
        in_specs=(P("row", "col", None), P("row", "col"), P("row", "col"), P()),
        out_specs=(P("row", "col", None), P("row", "col", None), P()),
        check_vma=False,
    )
```

```python
import jax
import jax.numpy as jnp
from jax import lax
from jax.experimental import pallas as pl
from jax.experimental.pallas import tpu as pltpu
from jax.sharding import PartitionSpec as P

STEP_ROWS = 16
CHUNK = 32
GROUP = 4
GROUPS = STEP_ROWS // GROUP
HALF = 128
HIGHEST = lax.Precision.HIGHEST
F32 = jnp.float32
BF16 = jnp.bfloat16


def over_pixels(left, right):
    return lax.dot_general(left, right, (((0,), (0,)), ((), ())), preferred_element_type=F32)


def exact(left, right, left_dim=1, right_dim=0):
    return lax.dot_general(
        left,
        right,
        (((left_dim,), (right_dim,)), ((), ())),
        precision=HIGHEST,
        preferred_element_type=F32,
    )


def split(value):
    high = value.astype(BF16)
    return high, (value - high.astype(F32)).astype(BF16)


def stacked_gains(gains):
    high = gains.astype(BF16)
    rest = gains - high.astype(F32)
    middle = rest.astype(BF16)
    low = (rest - middle.astype(F32)).astype(BF16)
    return jnp.concatenate([high, middle, low], 0)


def sends(pairs, sent, slot, start, groups=range(GROUPS)):
    return [
        pltpu.make_async_copy(
            buffer.at[slot, pl.ds(GROUP * group, GROUP)],
            target.at[pl.ds(start + GROUP * group, GROUP)],
            sent.at[which, slot, group],
        )
        for group in groups
        for which, (buffer, target) in enumerate(pairs)
    ]


def row_gains(classes, valid, gains, count):
    which = lax.rem(lax.broadcasted_iota(jnp.int32, (3 * count, classes.shape[1]), 0), count)
    onehot = jnp.where((which == classes) & (valid > 0), 1.0, 0.0).astype(BF16)
    return over_pixels(onehot, gains)


def as_column(row):
    return jnp.transpose(jnp.broadcast_to(row, (8, row.shape[1])))[:, :1]


def edges_kernel(row_ref, col_ref, class_ref, valid_ref, gains_ref, row_out, col_out):
    count = gains_ref.shape[0]
    gains = stacked_gains(gains_ref[...])
    cols = row_ref.shape[1]
    rows = col_ref.shape[0]
    calibrated = row_ref[0].astype(F32) * row_gains(class_ref[0:1, :], valid_ref[0:1, :], gains, count)
    row_out[0:cols, :] = calibrated
    row_out[cols:, :] = jnp.broadcast_to(valid_ref[0:1, :].astype(F32), (8, cols))
    which = lax.rem(lax.broadcasted_iota(jnp.int32, (rows, 3 * count), 1), count)
    first_valid = valid_ref[:, 0:1]
    onehot = jnp.where((which == class_ref[:, 0:1]) & (first_valid > 0), 1.0, 0.0).astype(BF16)
    gain_col = jnp.dot(onehot, gains, preferred_element_type=F32)
    channels = gain_col.shape[1]
    raw_col = col_ref[...].astype(F32)[:, 0, :]
    col_out[:, :channels] = raw_col * gain_col
    col_out[:, channels:] = jnp.broadcast_to(first_valid.astype(F32), (rows, 128))


def edges(raw_counts, gain_class, good_pixels, class_gains):
    rows, cols, channels = raw_counts.shape
    whole = lambda shape: pl.BlockSpec(shape, lambda i: (0,) * len(shape))
    return pl.pallas_call(
        edges_kernel,
        grid=(1,),
        in_specs=[
            whole((1, cols, channels)),
            whole((rows, 16, channels)),
            whole((rows, cols)),
            whole((rows, cols)),
            whole(class_gains.shape),
        ],
        out_specs=[whole((cols + 8, channels)), whole((rows, channels + 128))],
        out_shape=[
            jax.ShapeDtypeStruct((cols + 8, channels), F32),
            jax.ShapeDtypeStruct((rows, channels + 128), F32),
        ],
        name="edges",
    )(raw_counts, raw_counts, gain_class, good_pixels, class_gains)


def moments_kernel(
    raw_ref, class_ref, valid_ref, gains_ref, high_to, low_to, products_ref, sums_ref, pivot_ref, last_row_ref, last_col_ref, plain, half_degree, terms, gains_bf, high_ref, low_ref, sent
):
    step = pl.program_id(0)
    count = gains_ref.shape[0]
    rows, cols = valid_ref.shape
    channels = raw_ref.shape[2]

    @pl.when(step == 0)
    def _():
        valid = valid_ref[...].astype(F32)
        zero_row = jnp.zeros((1, cols), F32)
        zero_col = jnp.zeros((rows, 1), F32)
        degree = jnp.concatenate([valid[1:], zero_row], 0) + jnp.concatenate([zero_row, valid[:-1]], 0)
        degree = degree + jnp.concatenate([valid[:, 1:], zero_col], 1) + jnp.concatenate([zero_col, valid[:, :-1]], 1)
        half_degree[...] = 0.5 * degree
        plain[...] = jnp.zeros_like(plain)
        products_ref[...] = jnp.zeros_like(products_ref)
        sums_ref[...] = jnp.zeros_like(sums_ref)
        gains_bf[...] = stacked_gains(gains_ref[...])
        gain_map = row_gains(class_ref[0:1, :], valid_ref[0:1, :], gains_bf[...], count)
        number = jnp.maximum(jnp.sum(valid[0:1, :], keepdims=True), 1.0)
        pivot = jnp.sum(raw_ref[0].astype(F32) * gain_map, 0, keepdims=True) / number
        pivot_ref[...] = jnp.broadcast_to(pivot, pivot_ref.shape)

    start = pl.multiple_of(step * STEP_ROWS, STEP_ROWS)
    classes = class_ref[pl.ds(start, STEP_ROWS), :]
    valid = valid_ref[pl.ds(start, STEP_ROWS), :]
    slot = lax.rem(step, 2)
    pairs = ((high_ref, high_to), (low_ref, low_to))

    @pl.when(step >= 2)
    def _():
        for copy in sends(pairs, sent, slot, start - 2 * STEP_ROWS):
            copy.wait()

    degrees = jnp.transpose(half_degree[pl.ds(start, STEP_ROWS), :])
    valid_cols = jnp.transpose(valid.astype(F32))
    pivot = pivot_ref[0:1, :]
    gains = gains_bf[...]
    total = sums_ref[...]
    for row in range(STEP_ROWS):
        gain_map = row_gains(classes[row : row + 1], valid[row : row + 1], gains, count)
        for at in range(0, cols, CHUNK):
            calibrated = raw_ref[row, at : at + CHUNK, :].astype(F32) * gain_map[at : at + CHUNK]
            calibrated = calibrated - valid_cols[at : at + CHUNK, row : row + 1] * pivot
            high, low = split(calibrated)
            high_ref[slot, row, at : at + CHUNK, :] = high
            low_ref[slot, row, at : at + CHUNK, :] = low
            plain[row % 2, 8 + at : 8 + at + CHUNK, :] = calibrated
            left = plain[row % 2, 7 + at : 7 + at + CHUNK, :]
            above = plain[1 - row % 2, 8 + at : 8 + at + CHUNK, :]
            term = above + left - degrees[at : at + CHUNK, row : row + 1] * calibrated
            terms[row * cols + at : row * cols + at + CHUNK, :] = term.astype(BF16)
            total = total + jnp.sum(calibrated.reshape(CHUNK // 8, 8, channels), 0)
        last_col_ref[pl.ds(start + row, 1), :] = calibrated[CHUNK - 1 :, :]
        if row % GROUP == GROUP - 1:
            for copy in sends(pairs, sent, slot, start, [row // GROUP]):
                copy.start()
    sums_ref[...] = total
    last_row_ref[...] = plain[(STEP_ROWS - 1) % 2, 8:, :]
    pixels = STEP_ROWS * cols
    high = high_ref[slot].reshape(pixels, channels)
    products_ref[...] += over_pixels(high, jnp.concatenate([terms[...], high], 1))
    steps = rows // STEP_ROWS

    @pl.when(step == steps - 1)
    def _():
        if steps > 1:
            for copy in sends(pairs, sent, 1 - slot, start - STEP_ROWS):
                copy.wait()
        for copy in sends(pairs, sent, slot, start):
            copy.wait()


def moments(raw_counts, gain_class, good_pixels, class_gains):
    rows, cols, channels = raw_counts.shape
    whole = lambda shape: pl.BlockSpec(shape, lambda i: (0,) * len(shape))
    block = pl.BlockSpec((STEP_ROWS, cols, channels), lambda i: (i, 0, 0))
    pixels = rows * cols
    return pl.pallas_call(
        moments_kernel,
        grid=(rows // STEP_ROWS,),
        in_specs=[block, whole((rows, cols)), whole((rows, cols)), whole(class_gains.shape)],
        out_specs=[pl.BlockSpec(memory_space=pl.ANY)] * 2 + [whole((channels, 2 * channels)), whole((8, channels)), whole((8, channels)), whole((cols, channels)), whole((rows, channels))],
        out_shape=[
            pltpu.HBM(raw_counts.shape, BF16),
            pltpu.HBM(raw_counts.shape, BF16),
            jax.ShapeDtypeStruct((channels, 2 * channels), F32),
            jax.ShapeDtypeStruct((8, channels), F32),
            jax.ShapeDtypeStruct((8, channels), F32),
            jax.ShapeDtypeStruct((cols, channels), F32),
            jax.ShapeDtypeStruct((rows, channels), F32),
        ],
        scratch_shapes=[
            pltpu.VMEM((2, 8 + cols, channels), F32),
            pltpu.VMEM((rows, cols), F32),
            pltpu.VMEM((STEP_ROWS * cols, channels), BF16),
            pltpu.VMEM((3 * class_gains.shape[0], channels), BF16),
            pltpu.VMEM((2, STEP_ROWS, cols, channels), BF16),
            pltpu.VMEM((2, STEP_ROWS, cols, channels), BF16),
            pltpu.SemaphoreType.DMA((2, 2, GROUPS)),
        ],
        compiler_params=pltpu.CompilerParams(vmem_limit_bytes=32 * 1024 * 1024),
        cost_estimate=pl.CostEstimate(
            flops=10 * pixels * channels * channels, bytes_accessed=6 * pixels * channels, transcendentals=0
        ),
        name="moments",
    )(raw_counts, gain_class, good_pixels, class_gains)


def pack_kernel(
    products_ref, sums_ref, pivot_ref, below_ref, right_ref, last_row_ref, last_col_ref, valid_ref, packed_ref
):
    rows, cols = valid_ref.shape
    channels = sums_ref.shape[1]
    valid = valid_ref[...].astype(F32)
    last_valid = as_column(valid[rows - 1 : rows, :])
    below_row = below_ref[cols : cols + 1, :]
    below_valid = as_column(below_row)
    mine = last_row_ref[...]
    pivot = pivot_ref[0:1, :]
    down = last_valid * (below_ref[0:cols, :] - below_valid * pivot) - below_valid * mine
    right_valid = right_ref[:, channels : channels + 1]
    mine = last_col_ref[...]
    last_col = valid[:, cols - 1 : cols]
    right = last_col * (right_ref[:, :channels] - right_valid * pivot) - right_valid * mine
    edge = jnp.concatenate([down, right], 0).astype(BF16)
    cross = products_ref[:, :channels]
    noise = over_pixels(edge, edge) - (cross + jnp.transpose(cross))
    number = jnp.sum(valid, keepdims=True)
    total = jnp.sum(sums_ref[...], 0, keepdims=True)
    shift = total + number * pivot
    second = products_ref[:, channels:] + (as_column(pivot) * shift + as_column(total) * pivot)
    total = shift
    row = lax.broadcasted_iota(jnp.int32, (HALF, HALF), 0)
    col = lax.broadcasted_iota(jnp.int32, (HALF, HALF), 1)
    at = 0
    diagonals = []
    for matrix in (noise, second):
        packed_ref[at : at + HALF, :] = jnp.where(col <= row, matrix[:HALF, :HALF], matrix[HALF:, HALF:])
        packed_ref[at + HALF : at + 2 * HALF, :] = matrix[:HALF, HALF:]
        diagonals.append(jnp.sum(jnp.where(row == col, matrix[HALF:, HALF:], 0.0), 0, keepdims=True))
        at += 2 * HALF
    pairs = jnp.sum(valid[1:] * valid[:-1], keepdims=True) + jnp.sum(valid[:, 1:] * valid[:, :-1], keepdims=True)
    pairs = pairs + jnp.sum(valid[rows - 1 :] * below_row, keepdims=True)
    pairs = pairs + jnp.sum(last_col * right_valid, keepdims=True)
    line = lax.broadcasted_iota(jnp.int32, (8, HALF), 0)
    packed_ref[at : at + 8, :] = jnp.where(
        line == 0,
        total[:, :HALF],
        jnp.where(
            line == 1,
            total[:, HALF:],
            jnp.where(
                line == 2,
                number,
                jnp.where(
                    line == 3, pairs, jnp.where(line == 4, diagonals[0], jnp.where(line == 5, diagonals[1], 0.0))
                ),
            ),
        ),
    )
    if packed_ref.shape[0] > at + 8:
        packed_ref[at + 8 :, :] = jnp.zeros((packed_ref.shape[0] - at - 8, HALF), F32)


def pack(products, sums, pivot, below, right, last_row, last_col, good_pixels, length):
    rows, cols = good_pixels.shape
    whole = lambda shape: pl.BlockSpec(shape, lambda i: (0,) * len(shape))
    return pl.pallas_call(
        pack_kernel,
        grid=(1,),
        in_specs=[
            whole(products.shape),
            whole(sums.shape),
            whole(pivot.shape),
            whole(below.shape),
            whole(right.shape),
            whole(last_row.shape),
            whole(last_col.shape),
            whole((rows, cols)),
        ],
        out_specs=whole((length, HALF)),
        out_shape=jax.ShapeDtypeStruct((length, HALF), F32),
        compiler_params=pltpu.CompilerParams(vmem_limit_bytes=32 * 1024 * 1024),
        name="pack",
    )(products, sums, pivot, below, right, last_row, last_col, good_pixels)


def inverse_of_pair(a, b, c):
    scale = 1.0 / (a * c - b * b)
    return c * scale, -(b * scale), a * scale


def eliminate(jobs):
    lane = lax.broadcasted_iota(jnp.int32, (8, HALF), 1)
    line = lax.broadcasted_iota(jnp.int32, (8, HALF), 0)
    spread = lambda value: jnp.broadcast_to(value, (8, HALF))
    pick = lambda value, place: jnp.take_along_axis(
        value, jnp.full((8, HALF), place, jnp.int32), axis=1, mode="promise_in_bounds"
    )
    tiles = HALF // 8
    done = [([None] * tiles, [None] * tiles) for _ in jobs]
    for turn in range(HALF // 4):
        tile, first, at = turn // 2, 4 * (turn % 2), 4 * turn
        for job, (done_main, done_extra) in zip(jobs, done):
            main, extra = job["main"], job["extra"]
            lead = main[tile]
            rows = [spread(lead[first + i : first + i + 1, :]) for i in range(4)]
            p = {(i, j): pick(rows[i], at + j) for i in range(4) for j in range(i, 4)}
            if job["inverse"]:
                inside = (lane >= at) & (lane < at + 4)
                rows = [jnp.where(inside, jnp.where(lane == at + i, 1.0, 0.0), row) for i, row in enumerate(rows)]
            more = [spread(extra[tile][first + i : first + i + 1, :]) for i in range(4)] if extra else None
            e00, e01, e11 = inverse_of_pair(p[0, 0], p[0, 1], p[1, 1])
            f00 = e00 * p[0, 2] + e01 * p[1, 2]
            f10 = e01 * p[0, 2] + e11 * p[1, 2]
            f01 = e00 * p[0, 3] + e01 * p[1, 3]
            f11 = e01 * p[0, 3] + e11 * p[1, 3]
            g00, g01, g11 = inverse_of_pair(
                p[2, 2] - (p[0, 2] * f00 + p[1, 2] * f10),
                p[2, 3] - (p[0, 2] * f01 + p[1, 2] * f11),
                p[3, 3] - (p[0, 3] * f01 + p[1, 3] * f11),
            )
            i0 = lax.rsqrt(p[0, 0])
            l10, l20, l30 = p[0, 1] * i0, p[0, 2] * i0, p[0, 3] * i0
            i1 = lax.rsqrt(p[1, 1] - l10 * l10)
            l21, l31 = (p[1, 2] - l20 * l10) * i1, (p[1, 3] - l30 * l10) * i1
            i2 = lax.rsqrt(p[2, 2] - (l20 * l20 + l21 * l21))
            l32 = (p[2, 3] - (l30 * l20 + l31 * l21)) * i2
            i3 = lax.rsqrt(p[3, 3] - (l30 * l30 + l31 * l31 + l32 * l32))
            solved = []
            for group, target in ((rows, done_main), (more, done_extra)):
                if group is None:
                    solved.append(None)
                    continue
                u2 = group[2] - (f00 * group[0] + f10 * group[1])
                u3 = group[3] - (f01 * group[0] + f11 * group[1])
                z2 = g00 * u2 + g01 * u3
                z3 = g01 * u2 + g11 * u3
                z0 = (e00 * group[0] + e01 * group[1]) - (f00 * z2 + f01 * z3)
                z1 = (e01 * group[0] + e11 * group[1]) - (f10 * z2 + f11 * z3)
                solved.append((z0, z1, z2, z3))
                r0 = group[0] * i0
                r1 = (group[1] - l10 * r0) * i1
                r2 = (group[2] - (l20 * r0 + l21 * r1)) * i2
                r3 = (group[3] - (l30 * r0 + l31 * r1 + l32 * r2)) * i3
                quad = jnp.where(
                    line == first,
                    r0,
                    jnp.where(line == first + 1, r1, jnp.where(line == first + 2, r2, r3)),
                )
                target[tile] = quad if first == 0 else jnp.where(line < 4, target[tile], quad)
            for j in range(tile if first == 0 else tile + 1, tiles):
                weights = [spread(main[j][:, at + i : at + i + 1]) for i in range(4)]
                if j == tile:
                    weights = [jnp.where(line >= 4, weight, 0.0) for weight in weights]
                base = jnp.where(inside, 0.0, main[j]) if job["inverse"] else main[j]
                z = solved[0]
                main[j] = base - (
                    (weights[0] * z[0] + weights[1] * z[1]) + (weights[2] * z[2] + weights[3] * z[3])
                )
                if extra:
                    z = solved[1]
                    extra[j] = extra[j] - (
                        (weights[0] * z[0] + weights[1] * z[1]) + (weights[2] * z[2] + weights[3] * z[3])
                    )
    row = lax.broadcasted_iota(jnp.int32, (HALF, HALF), 0)
    col = lax.broadcasted_iota(jnp.int32, (HALF, HALF), 1)
    results = []
    for job, (done_main, done_extra) in zip(jobs, done):
        main = jnp.concatenate(done_main, 0)
        keep = (col <= row) if job["inverse"] else (col >= row)
        main = jnp.where(keep, main, 0.0)
        results.append((main, jnp.concatenate(done_extra, 0) if job["extra"] else None))
    return results


def tiles_of(matrix):
    return [matrix[8 * i : 8 * i + 8, :] for i in range(HALF // 8)]


def factors(packed_ref, pivot_ref, weights_ref, offset_ref, factor_ref):
    channels = 2 * HALF
    base = 4 * HALF
    line0 = packed_ref[base : base + 8, :]
    number = jnp.broadcast_to(line0[2:3, 0:1], (1, HALF))
    pairs = jnp.broadcast_to(line0[3:4, 0:1], (1, HALF))
    noise_scale = 1.0 / (2.0 * pairs)
    scale = 1.0 / number
    mean0, mean1 = line0[0:1] * scale, line0[1:2] * scale
    column0 = as_column(mean0)
    column1 = as_column(mean1)
    part = lambda i: packed_ref[HALF * i : HALF * (i + 1), :]
    row = lax.broadcasted_iota(jnp.int32, (HALF, HALF), 0)
    col = lax.broadcasted_iota(jnp.int32, (HALF, HALF), 1)

    def diagonal_blocks(block, diagonal):
        turned = jnp.transpose(block)
        lower = jnp.where(col <= row, block, turned)
        upper = jnp.where(col > row, block, turned)
        return lower, jnp.where(col == row, diagonal, upper)

    n00, n11 = (block * noise_scale for block in diagonal_blocks(part(0), line0[4:5]))
    n01 = part(1) * noise_scale
    s00, s11 = diagonal_blocks(part(2), line0[5:6])
    s00 = s00 * scale - column0 * mean0
    s01 = part(3) * scale - column0 * mean1
    s11 = s11 * scale - column1 * mean1
    (w00, y), (k00, k01) = eliminate(
        [
            dict(main=tiles_of(n00), extra=tiles_of(n01), inverse=True),
            dict(main=tiles_of(s00), extra=tiles_of(s01), inverse=False),
        ]
    )
    n11 = n11 - exact(y, y, 0, 0)
    s11 = s11 - exact(k01, k01, 0, 0)
    (w11, _), (k11, _) = eliminate(
        [
            dict(main=tiles_of(n11), extra=None, inverse=True),
            dict(main=tiles_of(s11), extra=None, inverse=False),
        ]
    )
    w10 = -exact(w11, exact(y, w00, 0, 0))
    factor_ref[:HALF, :HALF] = exact(k00, w00, 1, 1)
    factor_ref[:HALF, HALF:] = exact(k00, w10, 1, 1) + exact(k01, w11, 1, 1)
    factor_ref[HALF:, :HALF] = jnp.zeros((HALF, HALF), F32)
    factor_ref[HALF:, HALF:] = exact(k11, w11, 1, 1)
    mean0 = jnp.broadcast_to(mean0, (8, HALF)) - pivot_ref[:, :HALF]
    mean1 = jnp.broadcast_to(mean1, (8, HALF)) - pivot_ref[:, HALF:]
    offset_ref[:, :HALF] = exact(mean0, w00, 1, 1)
    offset_ref[:, HALF:] = exact(mean0, w10, 1, 1) + exact(mean1, w11, 1, 1)
    left = jnp.concatenate([jnp.transpose(w00), jnp.zeros((HALF, HALF), F32)], 0)
    right = jnp.concatenate([jnp.transpose(w10), jnp.transpose(w11)], 0)
    high, low = split(jnp.concatenate([left, right], 1))
    weights_ref[0:channels, :] = high
    weights_ref[channels : 2 * channels, :] = low
    weights_ref[2 * channels :, :] = high


def whiten_rows(high, low, weights):
    return jnp.dot(jnp.concatenate([high, high, low], 1), weights, preferred_element_type=F32)


def whiten_kernel(
    packed_ref,
    pivot_ref,
    high_from,
    low_from,
    valid_ref,
    below_ref,
    right_ref,
    white_to,
    noise_to,
    factor_ref,
    high_ref,
    low_ref,
    weights_ref,
    offset_ref,
    plain,
    right_edge,
    neighbours,
    arrived,
    white_ref,
    noise_ref,
    sent,
):
    step = pl.program_id(0)
    rows, cols = valid_ref.shape
    steps = rows // STEP_ROWS
    channels = high_ref.shape[2]

    @pl.when(step == 0)
    def _():
        valid = valid_ref[...].astype(F32)
        down = jnp.concatenate([valid[1:], below_ref[cols : cols + 1, :]], 0)
        right = jnp.concatenate([valid[:, 1:], right_ref[:, channels : channels + 1]], 1)
        neighbours[...] = down + right
        copies = [
            pltpu.make_async_copy(high_from, high_ref, arrived.at[0]),
            pltpu.make_async_copy(low_from, low_ref, arrived.at[1]),
        ]
        for copy in copies:
            copy.start()
        factors(packed_ref, pivot_ref, weights_ref, offset_ref, factor_ref)
        pivot = pivot_ref[0:1, :]
        below = below_ref[0:cols, :] - as_column(below_ref[cols : cols + 1, :]) * pivot
        plain[STEP_ROWS * (cols + 8) :, :] = whiten_rows(*split(below), weights_ref[...])
        right = right_ref[:, :channels] - right_ref[:, channels : channels + 1] * pivot
        right_edge[...] = whiten_rows(*split(right), weights_ref[...])
        for copy in copies:
            copy.wait()

    start = pl.multiple_of((steps - 1 - step) * STEP_ROWS, STEP_ROWS)
    slot = lax.rem(step, 2)
    pairs = ((white_ref, white_to), (noise_ref, noise_to))

    @pl.when(step >= 2)
    def _():
        for copy in sends(pairs, sent, slot, start + 2 * STEP_ROWS):
            copy.wait()

    valid = jnp.transpose(valid_ref[pl.ds(start, STEP_ROWS), :].astype(F32))
    number = jnp.transpose(neighbours[pl.ds(start, STEP_ROWS), :])
    edge = right_edge[pl.ds(start, STEP_ROWS), :]
    offset = offset_ref[0:1, :]
    weights = weights_ref[...]
    for row in reversed(range(STEP_ROWS)):
        base = row * (cols + 8)
        plain[base : base + cols, :] = whiten_rows(high_ref[start + row], low_ref[start + row], weights)
        plain[base + cols : base + cols + 1, :] = edge[row : row + 1]
        for at in range(0, cols, CHUNK):
            here = plain[base + at : base + at + CHUNK, :]
            right = plain[base + at + 1 : base + at + 1 + CHUNK, :]
            below = plain[base + cols + 8 + at : base + cols + 8 + at + CHUNK, :]
            ok = valid[at : at + CHUNK, row : row + 1]
            white_ref[slot, row, at : at + CHUNK, :] = (here - ok * offset).astype(BF16)
            around = number[at : at + CHUNK, row : row + 1]
            noise_ref[slot, row, at : at + CHUNK, :] = (ok * (below + right) - around * here).astype(BF16)
        if row % GROUP == 0:
            for copy in sends(pairs, sent, slot, start, [row // GROUP]):
                copy.start()
    plain[STEP_ROWS * (cols + 8) :, :] = plain[0 : cols, :]

    @pl.when(step == steps - 1)
    def _():
        if steps > 1:
            for copy in sends(pairs, sent, 1 - slot, start + STEP_ROWS):
                copy.wait()
        for copy in sends(pairs, sent, slot, start):
            copy.wait()


def whiten(packed, pivot, high, low, good_pixels, below, right):
    rows, cols, channels = high.shape
    steps = rows // STEP_ROWS
    pixels = rows * cols
    whole = lambda shape: pl.BlockSpec(shape, lambda i: (0,) * len(shape))
    return pl.pallas_call(
        whiten_kernel,
        grid=(steps,),
        in_specs=[
            whole(packed.shape),
            whole(pivot.shape),
            pl.BlockSpec(memory_space=pl.ANY),
            pl.BlockSpec(memory_space=pl.ANY),
            whole((rows, cols)),
            whole(below.shape),
            whole(right.shape),
        ],
        out_specs=[pl.BlockSpec(memory_space=pl.ANY)] * 2 + [whole((channels, channels))],
        out_shape=[jax.ShapeDtypeStruct(high.shape, BF16)] * 2 + [jax.ShapeDtypeStruct((channels, channels), F32)],
        scratch_shapes=[
            pltpu.VMEM(high.shape, BF16),
            pltpu.VMEM(low.shape, BF16),
            pltpu.VMEM((3 * channels, channels), BF16),
            pltpu.VMEM((8, channels), F32),
            pltpu.VMEM((STEP_ROWS * (cols + 8) + cols, channels), F32),
            pltpu.VMEM((rows, channels), F32),
            pltpu.VMEM((rows, cols), F32),
            pltpu.SemaphoreType.DMA((2,)),
            pltpu.VMEM((2, STEP_ROWS, cols, channels), BF16),
            pltpu.VMEM((2, STEP_ROWS, cols, channels), BF16),
            pltpu.SemaphoreType.DMA((2, 2, GROUPS)),
        ],
        compiler_params=pltpu.CompilerParams(vmem_limit_bytes=48 * 1024 * 1024),
        cost_estimate=pl.CostEstimate(
            flops=6 * pixels * channels * channels, bytes_accessed=8 * pixels * channels, transcendentals=0
        ),
        name="whiten",
    )(packed, pivot, high, low, good_pixels, below, right)


def from_next(value, axis):
    count = lax.axis_size(axis)
    return lax.ppermute(value, axis, [(source, source - 1) for source in range(1, count)])


def summed(packed):
    axes = ("col", "row")
    cols, rows = (lax.axis_size(axis) for axis in axes)
    core = lax.axis_index("row") % 2
    swap = [(i, i ^ 1) for i in range(rows)]
    groups = [[c * rows + r for c in range(cols) for r in range(k, rows, 2)] for k in range(2)]
    peers = cols * rows // 2
    parts = packed.reshape(2, packed.shape[0] // 2, HALF)
    kept = lax.dynamic_index_in_dim(parts, core, 0, keepdims=False)
    given = lax.dynamic_index_in_dim(parts, 1 - core, 0, keepdims=False)
    share = (kept + lax.ppermute(given, "row", swap)).reshape(peers, -1, 1, HALF)
    mine = jnp.sum(lax.all_to_all(share, axes, 0, 0, axis_index_groups=groups), 0)
    every = lax.all_to_all(jnp.broadcast_to(mine[None], share.shape), axes, 0, 0, axis_index_groups=groups)
    every = every.reshape(kept.shape)
    other = lax.ppermute(every, "row", swap)
    return jnp.concatenate([jnp.where(core == 0, every, other), jnp.where(core == 0, other, every)], 0)


def on_device(raw_counts, gain_class, good_pixels, class_gains):
    raw_counts = pltpu.with_memory_space_constraint(raw_counts, pltpu.HBM)
    first_row, first_col = edges(raw_counts, gain_class, good_pixels, class_gains)
    below = from_next(first_row, "row")
    right = from_next(first_col, "col")
    high, low, products, sums, pivot, last_row, last_col = moments(raw_counts, gain_class, good_pixels, class_gains)
    high, low = (pltpu.with_memory_space_constraint(part, pltpu.HBM) for part in (high, low))
    devices = lax.axis_size(("col", "row"))
    length = -(-(4 * HALF + 8) // devices) * devices
    packed = pack(products, sums, pivot, below, right, last_row, last_col, good_pixels, length)
    return whiten(summed(packed), pivot, high, low, good_pixels, below, right)


def solution(mesh):
    return jax.shard_map(
        on_device,
        mesh=mesh,
        in_specs=(P("row", "col", None), P("row", "col"), P("row", "col"), P()),
        out_specs=(P("row", "col", None), P("row", "col", None), P()),
        check_vma=False,
    )
```
